32 devices in a mesh: fsdp: 2 (over y), tensor: 8 (over z, x), ctx: 2 (over core).
Axes of the slice: x: 2, y: 2, z: 4, core: 2. Of those that a mesh axis runs over, the one named last changes fastest.
Arguments:
- hidden_in: bfloat16 [16, 2048, 1024], P('fsdp', ('tensor', 'ctx')), may hold values from -6 to 6
- segment_ids: int32 [16, 2048], P('fsdp'), may hold values from 0 to 3, never falling along the last dimension, each value on 1 to 1024 neighbouring positions
- norm_gains: bfloat16 [2, 1024], replicated, may hold values from 0.5 to 1.5
- norm_biases: bfloat16 [2, 1024], replicated, may hold values from -1.75 to 1.75
- qkv_weight: bfloat16 [1024, 16, 192], P(('fsdp', 'ctx'), 'tensor'), may hold values from -0.1875 to 0.1875
- qkv_bias: bfloat16 [16, 192], P('tensor'), may hold values from -1.75 to 1.75
- dense_weight: bfloat16 [16, 64, 1024], P('tensor', None, ('fsdp', 'ctx')), may hold values from -2 to 2
- fc_in_weight: bfloat16 [1024, 4096], P(('fsdp', 'ctx'), 'tensor'), may hold values from -0.1875 to 0.1875
- fc_in_bias: bfloat16 [4096], P('tensor'), may hold values from -3 to 3
- fc_out_weight: bfloat16 [4096, 1024], P('tensor', ('fsdp', 'ctx')), may hold values from -0.09375 to 0.09375
- out_biases: bfloat16 [2, 1024], replicated, may hold values from -1.75 to 1.75
- out_grad: bfloat16 [16, 2048, 1024], P('fsdp', ('tensor', 'ctx')), may hold values from -6 to 6
Outputs:
- hidden_out: bfloat16 [16, 2048, 1024], P('fsdp', ('tensor', 'ctx'))
- input_grad: bfloat16 [16, 2048, 1024], P('fsdp', ('tensor', 'ctx'))
- gain_grads: float32 [2, 1024], replicated
- norm_bias_grads: float32 [2, 1024], replicated
- qkv_weight_grad: float32 [1024, 16, 192], P(('fsdp', 'ctx'), 'tensor')
- qkv_bias_grad: float32 [16, 192], P('tensor')
- dense_weight_grad: float32 [16, 64, 1024], P('tensor', None, ('fsdp', 'ctx'))
- fc_in_weight_grad: float32 [1024, 4096], P(('fsdp', 'ctx'), 'tensor')
- fc_in_bias_grad: float32 [4096], P('tensor')
- fc_out_weight_grad: float32 [4096, 1024], P('tensor', ('fsdp', 'ctx'))
- out_bias_grads: float32 [2, 1024], replicated
The draws below stay inside these ranges and needn't reach their ends.
Inputs may be any that keep to these rules, and one draw needn't show every extreme that they name: `segment_ids`: along each sequence the numbers never fall; each of 0 to 3 covers 1 to 1024 positions, and one covers exactly 1024.
All inputs are finite; a program needn't handle non-finite values.
Results may differ from the reference program's by a relative error of at most 0.011.
Values may be sent and summed in bfloat16 or wider, within the bound.
No kernel may reach another device: no remote copies, remote signals or barrier semaphores. Data moves between devices by JAX's collectives and lax.ppermute only.
A program may use at most 256 MiB of HBM per device.

```python
import math
import jax
import jax.numpy as jnp
import numpy as np
from jax import lax

D = 1024
FF = 4096
HEADS = 16
HD = 64
ROT = 16
LEN = 2048
DOCS = 4
SEQS = 16


def level_of(stream_key, dims, cuts, low, largest):
    factor_of = 1.0
    for position, blocks in cuts:
        steps = jax.random.uniform(jax.random.fold_in(jax.random.fold_in(stream_key, 6), position), (blocks,), jnp.float32, low / len(cuts), largest / len(cuts))
        factor_of = factor_of * jnp.repeat(jnp.exp(steps), dims[position] // blocks).reshape((-1,) + (1,) * (len(dims) - 1 - position))
    return factor_of


def profile(number_of, total, bound, skew):
    weights = [(1 << 20) // math.isqrt(rank ** skew) + 1 for rank in range(2, number_of + 1)]
    spare, counts = total - bound - (number_of - 1), [1] * (number_of - 1)
    while spare > 0:
        movable = [i for i in range(number_of - 1) if counts[i] < bound]
        whole, remaining = sum([weights[i] for i in movable]), spare
        for i in movable:
            more = min(bound - counts[i], max(1, remaining * weights[i] // whole), spare)
            counts[i] = counts[i] + more
            spare = spare - more
    return np.array([bound] + counts)


def ragged_sizes(key, number_of, total, most, skew):
    if number_of == 2:
        one = jax.random.randint(key, (), max(1, total - most), min(most, total - 1) + 1)
        return jnp.stack([one, total - one])
    tallies = jnp.asarray(profile(number_of, total, most, skew), jnp.int32)
    pairs = (number_of - 1) // 2
    donor, taker = tallies[1:1 + 2 * pairs:2], tallies[2:2 + 2 * pairs:2]
    room = jnp.minimum(donor - 1, most - taker)
    shifted = jax.random.randint(jax.random.fold_in(key, 1), (pairs,), 0, 1 << 20) % (room + 1)
    tallies = tallies.at[1:1 + 2 * pairs:2].set(donor - shifted).at[2:2 + 2 * pairs:2].set(taker + shifted)
    return tallies[jax.random.permutation(jax.random.fold_in(key, 2), number_of)]


def gaussian(stream_key, dims, width, most, cuts=(), kind=jnp.bfloat16):
    drawn = jax.random.normal(stream_key, dims, jnp.float32) * width
    if len(cuts) > 0:
        drawn = level_of(stream_key, dims, cuts, -0.22, 0.18) * drawn
    return jnp.clip(drawn, min=-most, max=most).astype(kind)


def setup_inputs(seed: int = 0) -> dict:
    splits = jax.random.split(jax.random.key(seed), 13)
    hidden_in = gaussian(splits[0], (SEQS, LEN, D), 1.0, 6.0, ((0, 2), (1, 16)))
    segment_ids = jax.vmap(lambda own: jnp.searchsorted(jnp.cumsum(ragged_sizes(own, DOCS, LEN, LEN // 2, 2)), jnp.arange(LEN), side="right"))(jax.random.split(splits[1], SEQS)).reshape((SEQS, LEN)).astype(jnp.int32)
    norm_gains = jnp.clip(1.0 + 0.1 * jax.random.normal(splits[2], (2, D), jnp.float32), 0.5, 1.5).astype(jnp.bfloat16)
    norm_biases = gaussian(splits[3], (2, D), 0.3, 1.75)
    qkv_weight = gaussian(splits[4], (D, HEADS, 3 * HD), D ** -0.5, 0.1875, ((0, 4), (1, 8)))
    qkv_bias = gaussian(splits[5], (HEADS, 3 * HD), 0.3, 1.75, ((0, 8),))
    dense_weight = gaussian(splits[6], (HEADS, HD, D), (max(1, HEADS * HD * 16 // LEN)) ** -0.5, 2.0, ((0, 8), (2, 4)))
    fc_in_weight = gaussian(splits[7], (D, FF), D ** -0.5, 0.1875, ((0, 4), (1, 8)))
    fc_in_bias = gaussian(splits[8], (FF,), 0.5, 3.0, ((0, 8),))
    fc_out_weight = gaussian(splits[9], (FF, D), FF ** -0.5, 0.09375, ((0, 8), (1, 4)))
    out_biases = gaussian(splits[10], (2, D), 0.3, 1.75)
    out_grad = gaussian(splits[11], (SEQS, LEN, D), 1.0, 6.0, ((0, 2), (1, 16)))
    return {"hidden_in": hidden_in, "segment_ids": segment_ids, "norm_gains": norm_gains, "norm_biases": norm_biases, "qkv_weight": qkv_weight, "qkv_bias": qkv_bias, "dense_weight": dense_weight, "fc_in_weight": fc_in_weight, "fc_in_bias": fc_in_bias, "fc_out_weight": fc_out_weight, "out_biases": out_biases, "out_grad": out_grad}


@jax.custom_vjp
def low(v):
    return lax.optimization_barrier(v.astype(jnp.bfloat16)).astype(jnp.float32)

@jax.custom_vjp
def low_back(v):
    return v

def low_keep(v):
    return (low(v), None)

def low_pass(kept, grad):
    return (grad,)

def back_keep(v):
    return (v, None)

def back_low(kept, grad):
    return (low(grad),)
low.defvjp(low_keep, low_pass)
low_back.defvjp(back_keep, back_low)
highest = lax.Precision.HIGHEST
epsilon = 1e-05

def layer_norm(values, gain_row, shift_row):
    center = values - lax.optimization_barrier(jnp.mean(values, axis=-1, keepdims=True))
    inverse = lax.rsqrt(lax.optimization_barrier(jnp.mean(center * center, axis=-1, keepdims=True)) + epsilon)
    return center * inverse * gain_row + shift_row

def rotary_tables(segments):
    places = jnp.arange(LEN, dtype=jnp.int32)
    change = jnp.concatenate([jnp.ones((1,), jnp.int32), (segments[1:] != segments[:-1]).astype(jnp.int32)])
    starts = lax.cummax(places * change, axis=0)
    relative = (places - starts).astype(jnp.float32)
    freqs = 10000.0 ** (-jnp.arange(0, ROT, 2, dtype=jnp.float32) / ROT)
    angle = relative[:, None] * freqs[None, :]
    angle = jnp.concatenate([angle, angle], axis=-1)
    return (jnp.cos(angle), jnp.sin(angle))

def rotate(values, cosine, sine_part):
    half_size = ROT // 2
    head_part = values[..., :ROT]
    turned = jnp.concatenate([-head_part[..., half_size:], head_part[..., :half_size]], axis=-1)
    return jnp.concatenate([head_part * cosine + turned * sine_part, values[..., ROT:]], axis=-1)

def one_sequence(rows_in, segments, params):
    gain_rows, shift_rows, w_qkv, b_qkv, w_dense, w_in, b_in, w_out, bias_rows = params
    first_norm = low(layer_norm(rows_in, gain_rows[0], shift_rows[0]))
    second_norm = low(layer_norm(rows_in, gain_rows[1], shift_rows[1]))
    qkv_all = low_back(jnp.einsum('td,dhe->the', first_norm, w_qkv, precision=highest) + b_qkv)
    cosine, sine_part = rotary_tables(segments)
    cosine = cosine[:, None, :]
    sine_part = sine_part[:, None, :]
    queries = low(rotate(qkv_all[..., :HD], cosine, sine_part))
    keys_rot = low(rotate(qkv_all[..., HD:2 * HD], cosine, sine_part))
    values_in = low(qkv_all[..., 2 * HD:])
    scores = low_back(jnp.einsum('qhe,khe->hqk', queries, keys_rot, precision=highest) * HD ** (-0.5))
    places = jnp.arange(LEN, dtype=jnp.int32)
    allowed = (segments[:, None] == segments[None, :]) & (places[None, :] <= places[:, None])
    masked = jnp.where(allowed[None], scores, -1e+30)
    top_score = lax.optimization_barrier(jnp.max(masked, axis=-1, keepdims=True))
    exp_values = jnp.exp(masked - top_score)
    prob_low = low(exp_values / lax.optimization_barrier(jnp.sum(exp_values, axis=-1, keepdims=True)))
    attended = low(low_back(jnp.einsum('hqk,khe->qhe', prob_low, values_in, precision=highest)))
    attn_out = jnp.einsum('qhe,hed->qd', attended, w_dense, precision=highest)
    preact = low_back(jnp.dot(second_norm, w_in, precision=highest) + b_in)
    active = low(jax.nn.gelu(preact, approximate=False))
    mlp_out = jnp.dot(active, w_out, precision=highest)
    return rows_in + attn_out + mlp_out + bias_rows[0] + bias_rows[1]

def reference(hidden_in, segment_ids, norm_gains, norm_biases, qkv_weight, qkv_bias, dense_weight, fc_in_weight, fc_in_bias, fc_out_weight, out_biases, out_grad):
    params = tuple((item_in.astype(jnp.float32) for item_in in (norm_gains, norm_biases, qkv_weight, qkv_bias, dense_weight, fc_in_weight, fc_in_bias, fc_out_weight, out_biases)))
    rows_all = hidden_in.astype(jnp.float32)
    group_count = SEQS
    seg_groups = segment_ids.reshape(group_count, 1, LEN)

    def forward(param_set, rows_in):

        def group_step(carry, block_item):
            group_rows, group_segs = block_item
            result = jax.vmap(one_sequence, in_axes=(0, 0, None))(group_rows, group_segs, param_set)
            return (carry, result)
        _, result = lax.scan(jax.checkpoint(group_step), jnp.zeros((), jnp.float32), (rows_in.reshape(group_count, 1, LEN, D), seg_groups))
        return result.reshape(SEQS, LEN, D)
    result, pullback = jax.vjp(forward, params, rows_all)
    grads, grad_rows = pullback(out_grad.astype(jnp.float32))
    return (result.astype(jnp.bfloat16), grad_rows.astype(jnp.bfloat16), grads[0], grads[1], grads[2], grads[3], grads[4], grads[5], grads[6], grads[7], grads[8])
```

```python
import functools

import jax
import jax.numpy as jnp
from jax import lax
from jax.experimental import pallas as pl
from jax.experimental.pallas import tpu as pltpu
from jax.sharding import PartitionSpec as P

HD = 64
ROT = 16
PAIR = 2 * HD
TILE = 256
SPAN = 1024
EVERY = ("fsdp", "tensor", "ctx")
CHIPS = ("fsdp", "tensor")
BF = jnp.bfloat16
F32 = jnp.float32
epsilon = 1e-05
VMEM = 56 * 1024 * 1024


def nt(a, b):
    return lax.dot_general(a, b, (((1,), (1,)), ((), ())), preferred_element_type=F32)


def nn(a, b):
    return jnp.dot(a, b, preferred_element_type=F32)


def tn(a, b):
    return lax.dot_general(a, b, (((0,), (0,)), ((), ())), preferred_element_type=F32)


def params(*kinds):
    return pltpu.CompilerParams(dimension_semantics=kinds, vmem_limit_bytes=VMEM)


def cost(flops, moved, special=0):
    return pl.CostEstimate(flops=int(flops), bytes_accessed=int(moved), transcendentals=int(special))


def layer_stats(values):
    center = values - jnp.mean(values, axis=-1, keepdims=True)
    inverse = lax.rsqrt(jnp.mean(center * center, axis=-1, keepdims=True) + epsilon)
    return (center * inverse, inverse)


def norms_kernel(x_ref, gain_ref, shift_ref, one_ref, two_ref):
    normed, _ = layer_stats(x_ref[...].astype(F32))
    one_ref[...] = (normed * gain_ref[0:1, :] + shift_ref[0:1, :]).astype(BF)
    two_ref[...] = (normed * gain_ref[1:2, :] + shift_ref[1:2, :]).astype(BF)


def norms_call(x, gains, shifts):
    tokens, feats = x.shape
    row = pl.BlockSpec((TILE, feats), lambda i: (i, 0))
    pair = pl.BlockSpec((2, feats), lambda i: (0, 0))
    return pl.pallas_call(
        norms_kernel,
        grid=(tokens // TILE,),
        in_specs=[row, pair, pair],
        out_specs=[row, row],
        out_shape=[jax.ShapeDtypeStruct((tokens, feats), BF)] * 2,
        compiler_params=params("arbitrary"),
        cost_estimate=cost(tokens * feats * 12, tokens * feats * 6),
        name="norms",
    )(x, gains, shifts)


def qkv_kernel(one_ref, w_ref, bias_ref, cos_ref, sin_ref, out_ref):
    width = w_ref.shape[0] // 3
    lane = lax.broadcasted_iota(jnp.int32, (TILE, PAIR), 1) % HD
    low_half = lane < ROT // 2
    cosine = cos_ref[...]
    sine_part = sin_ref[...]
    rows = one_ref[...]
    for part in range(3):
        span = slice(part * width, (part + 1) * width)
        whole = nt(rows, w_ref[span, :]) + bias_ref[:, span]
        if part == 2:
            out_ref[:, span] = whole.astype(BF)
            continue
        for first in range(0, width, PAIR):
            u = whole[:, first : first + PAIR]
            turned = jnp.where(
                low_half, pltpu.roll(u, PAIR - ROT // 2, 1), pltpu.roll(u, ROT // 2, 1)
            )
            u = u * cosine + turned * sine_part
            if part == 0:
                u = u * HD ** (-0.5)
            out_ref[:, part * width + first : part * width + first + PAIR] = u.astype(BF)


def qkv_call(one, w, bias, cosine, sine_part):
    tokens, feats = one.shape
    cols = w.shape[0]
    return pl.pallas_call(
        qkv_kernel,
        grid=(tokens // TILE,),
        in_specs=[
            pl.BlockSpec((TILE, feats), lambda i: (i, 0)),
            pl.BlockSpec((cols, feats), lambda i: (0, 0)),
            pl.BlockSpec((1, cols), lambda i: (0, 0)),
            pl.BlockSpec((TILE, PAIR), lambda i: (i, 0)),
            pl.BlockSpec((TILE, PAIR), lambda i: (i, 0)),
        ],
        out_specs=pl.BlockSpec((TILE, cols), lambda i: (i, 0)),
        out_shape=jax.ShapeDtypeStruct((tokens, cols), BF),
        compiler_params=params("arbitrary"),
        cost_estimate=cost(2 * tokens * feats * cols, 2 * (tokens * (feats + cols) + feats * cols)),
        name="qkv",
    )(one, w, bias, cosine, sine_part)


def turn_back(g, cosine, sine_part):
    eight = ROT // 2
    parts = []
    for head in range(2):
        own = g[head * HD : (head + 1) * HD]
        low, high = own[:eight], own[eight:ROT]
        parts += [low * cosine + high * sine_part, high * cosine - low * sine_part, own[ROT:]]
    return jnp.concatenate(parts, axis=0)


def attend_kernel(
    begin_ref,
    q_ref,
    k_ref,
    v_ref,
    grad_ref,
    doc_ref,
    cos_ref,
    sin_ref,
    att_ref,
    dq_ref,
    dk_ref,
    dv_ref,
    score_ref,
    prob_ref,
    key_turn_ref,
    value_turn_ref,
    dk_sum_ref,
    dv_sum_ref,
):
    tile = pl.program_id(1)
    tiles = pl.num_programs(1)
    total_tiles = k_ref.shape[0] // TILE

    @pl.when(tile == 0)
    def _():
        dk_sum_ref[...] = jnp.zeros_like(dk_sum_ref)
        dv_sum_ref[...] = jnp.zeros_like(dv_sum_ref)

        def turn(block, _):
            rows = pl.ds(pl.multiple_of(block * TILE, TILE), TILE)
            key_turn_ref[block] = k_ref[rows, :].astype(F32).T.astype(BF)
            value_turn_ref[block] = v_ref[rows, :].astype(F32).T.astype(BF)
            return 0

        lax.fori_loop(0, total_tiles, turn, 0)

    lane = lax.broadcasted_iota(jnp.int32, (TILE, PAIR), 1)
    q_wide = q_ref[...].astype(F32)
    g_wide = grad_ref[...].astype(F32)
    q_heads = [
        jnp.where(lane < HD, q_wide, 0.0).astype(BF),
        jnp.where(lane >= HD, q_wide, 0.0).astype(BF),
    ]
    g_heads = [
        jnp.where(lane < HD, g_wide, 0.0).astype(BF),
        jnp.where(lane >= HD, g_wide, 0.0).astype(BF),
    ]
    first = begin_ref[tile]
    doc = doc_ref[0]
    key_place = lax.broadcasted_iota(jnp.int32, (TILE, TILE), 0)
    query_place = lax.broadcasted_iota(jnp.int32, (TILE, TILE), 1) + tile * TILE

    def rows_of(block):
        return pl.ds(pl.multiple_of(block * TILE, TILE), TILE)

    def scores_step(block, tops):
        keys = k_ref[rows_of(block), :]
        place = key_place + block * TILE
        allowed = (place >= doc) & (place <= query_place)
        new = []
        for head in range(2):
            s = jnp.where(allowed, nt(keys, q_heads[head]), -1e30)
            score_ref[head, rows_of(block - first), :] = s
            new.append(jnp.maximum(tops[head], jnp.max(s, axis=0, keepdims=True)))
        return tuple(new)

    lowest = jnp.full((1, TILE), -1e30, F32)
    tops = lax.fori_loop(first, tile + 1, scores_step, (lowest, lowest))

    def exp_step(block, sums):
        values = v_ref[rows_of(block), :]
        new = []
        for head in range(2):
            e = jnp.exp(score_ref[head, rows_of(block - first), :] - tops[head])
            score_ref[head, rows_of(block - first), :] = e
            gp = nt(values, g_heads[head])
            prob_ref[head, rows_of(block - first), :] = gp
            new.append(sums[2 * head] + jnp.sum(e, axis=0, keepdims=True))
            new.append(sums[2 * head + 1] + jnp.sum(e * gp, axis=0, keepdims=True))
        return tuple(new)

    none = jnp.zeros((1, TILE), F32)
    sums = lax.fori_loop(first, tile + 1, exp_step, (none,) * 4)
    inverse = [1.0 / sums[0], 1.0 / sums[2]]
    means = [sums[1] * inverse[0], sums[3] * inverse[1]]

    def grad_step(block, turned):
        new = []
        dk = dk_sum_ref[rows_of(block), :]
        dv = dv_sum_ref[rows_of(block), :]
        for head in range(2):
            p = score_ref[head, rows_of(block - first), :] * inverse[head]
            gs = (p * (prob_ref[head, rows_of(block - first), :] - means[head])).astype(BF)
            p_low = p.astype(BF)
            dv = dv + nn(p_low, g_heads[head])
            dk = dk + nn(gs, q_heads[head])
            half = slice(head * HD, (head + 1) * HD)
            new.append(turned[2 * head] + nn(value_turn_ref[block, half, :], p_low))
            new.append(turned[2 * head + 1] + nn(key_turn_ref[block, half, :], gs))
        dk_sum_ref[rows_of(block), :] = dk
        dv_sum_ref[rows_of(block), :] = dv
        return tuple(new)

    flat = jnp.zeros((HD, TILE), F32)
    turned = lax.fori_loop(first, tile + 1, grad_step, (flat,) * 4)
    att_ref[...] = jnp.concatenate([turned[0], turned[2]], axis=0).T.astype(BF)
    dq = jnp.concatenate([turned[1], turned[3]], axis=0) * HD ** (-0.5)
    dq_ref[...] = turn_back(dq, cos_ref[tile], sin_ref[tile]).T.astype(BF)

    @pl.when(tile == tiles - 1)
    def _():
        dv_ref[...] = dv_sum_ref[...].astype(BF)

        def finish(block, _):
            g = dk_sum_ref[rows_of(block), :].T
            dk_ref[rows_of(block), :] = turn_back(g, cos_ref[block], sin_ref[block]).T.astype(BF)
            return 0

        lax.fori_loop(0, total_tiles, finish, 0)


def attend_call(begin, qkv, grad_att, doc, cosine, sine_part):
    tokens = qkv.shape[0]
    width = qkv.shape[1] // 3
    pairs = width // PAIR
    tiles = tokens // TILE
    reach = SPAN + TILE
    query = pl.BlockSpec((TILE, PAIR), lambda p, i, *_: (i, p))
    whole = pl.BlockSpec((tokens, PAIR), lambda p, i, *_: (0, p))
    table = pl.BlockSpec((tiles, ROT // 2, TILE), lambda p, i, *_: (0, 0, 0))
    return pl.pallas_call(
        attend_kernel,
        grid_spec=pltpu.PrefetchScalarGridSpec(
            num_scalar_prefetch=1,
            grid=(pairs, tiles),
            in_specs=[
                query,
                pl.BlockSpec((tokens, PAIR), lambda p, i, *_: (0, pairs + p)),
                pl.BlockSpec((tokens, PAIR), lambda p, i, *_: (0, 2 * pairs + p)),
                query,
                pl.BlockSpec((1, 1, TILE), lambda p, i, *_: (i, 0, 0)),
                table,
                table,
            ],
            out_specs=[query, query, whole, whole],
            scratch_shapes=[
                pltpu.VMEM((2, reach, TILE), F32),
                pltpu.VMEM((2, reach, TILE), F32),
                pltpu.VMEM((tiles, PAIR, TILE), BF),
                pltpu.VMEM((tiles, PAIR, TILE), BF),
                pltpu.VMEM((tokens, PAIR), F32),
                pltpu.VMEM((tokens, PAIR), F32),
            ],
        ),
        out_shape=[jax.ShapeDtypeStruct((tokens, width), BF)] * 4,
        compiler_params=params("arbitrary", "arbitrary"),
        cost_estimate=cost(
            tokens * 800 * width * 4 * 12, tokens * width * 16, tokens * 600 * (width // HD)
        ),
        name="attend",
    )(begin, qkv, qkv, qkv, grad_att, doc, cosine, sine_part)


def units_kernel(two_ref, dy_ref, win_ref, wout_ref, bias_ref, act_ref, pre_ref, sum_ref):
    pre = nt(two_ref[...], win_ref[...]) + bias_ref[...]
    upstream = nt(dy_ref[...], wout_ref[...])
    cdf = 0.5 * (1.0 + lax.erf(pre * 0.7071067811865476))
    density = jnp.exp(-0.5 * pre * pre) * 0.3989422804014327
    act_ref[...] = (pre * cdf).astype(BF)
    back = (upstream * (cdf + pre * density)).astype(BF)
    pre_ref[...] = back

    @pl.when(pl.program_id(1) == 0)
    def _():
        sum_ref[...] = jnp.zeros_like(sum_ref)

    sum_ref[...] += jnp.sum(back.astype(F32), axis=0, keepdims=True)


def units_call(two, dy, w_in, w_out, bias):
    tokens, feats = two.shape
    units = w_in.shape[0]
    step = 512
    row = pl.BlockSpec((TILE, feats), lambda j, i: (i, 0))
    weight = pl.BlockSpec((step, feats), lambda j, i: (j, 0))
    line = pl.BlockSpec((1, step), lambda j, i: (0, j))
    out = pl.BlockSpec((TILE, step), lambda j, i: (i, j))
    return pl.pallas_call(
        units_kernel,
        grid=(units // step, tokens // TILE),
        in_specs=[row, row, weight, weight, line],
        out_specs=[out, out, line],
        out_shape=[
            jax.ShapeDtypeStruct((tokens, units), BF),
            jax.ShapeDtypeStruct((tokens, units), BF),
            jax.ShapeDtypeStruct((1, units), F32),
        ],
        compiler_params=params("arbitrary", "arbitrary"),
        cost_estimate=cost(
            4 * tokens * feats * units, 40 * tokens * feats, 2 * tokens * units
        ),
        name="units",
    )(two, dy, w_in, w_out, bias)


def output_kernel(att_ref, act_ref, wd_ref, wout_ref, out_ref):
    out_ref[...] = (nn(att_ref[...], wd_ref[...]) + nn(act_ref[...], wout_ref[...])).astype(BF)


def output_call(att, act, w_dense, w_out):
    tokens, width = att.shape
    units, feats = w_out.shape
    return pl.pallas_call(
        output_kernel,
        grid=(tokens // TILE,),
        in_specs=[
            pl.BlockSpec((TILE, width), lambda i: (i, 0)),
            pl.BlockSpec((TILE, units), lambda i: (i, 0)),
            pl.BlockSpec((width, feats), lambda i: (0, 0)),
            pl.BlockSpec((units, feats), lambda i: (0, 0)),
        ],
        out_specs=pl.BlockSpec((TILE, feats), lambda i: (i, 0)),
        out_shape=jax.ShapeDtypeStruct((tokens, feats), BF),
        compiler_params=params("arbitrary"),
        cost_estimate=cost(
            2 * tokens * feats * (width + units),
            2 * (tokens * (width + units + feats) + feats * (width + units)),
        ),
        name="output",
    )(att, act, w_dense, w_out)


def back_kernel(
    dq_ref, dk_ref, dv_ref, pre_ref, x_ref, wq_ref, win_ref, gain_ref, out_ref, stat_ref, bias_ref
):
    width = dq_ref.shape[1]
    parts = [dq_ref[...], dk_ref[...], dv_ref[...]]
    one = nn(parts[0], wq_ref[:width, :])
    one += nn(parts[1], wq_ref[width : 2 * width, :])
    one += nn(parts[2], wq_ref[2 * width :, :])
    two = nn(pre_ref[...], win_ref[...])
    normed, _ = layer_stats(x_ref[...].astype(F32))
    out_ref[...] = (one * gain_ref[0:1, :] + two * gain_ref[1:2, :]).astype(BF)

    @pl.when(pl.program_id(0) == 0)
    def _():
        stat_ref[...] = jnp.zeros_like(stat_ref)
        bias_ref[...] = jnp.zeros_like(bias_ref)

    for row, value in enumerate((one * normed, two * normed, one, two)):
        stat_ref[row : row + 1, :] += jnp.sum(value, axis=0, keepdims=True)
    for row in range(3):
        span = slice(row * width, (row + 1) * width)
        bias_ref[:, span] += jnp.sum(parts[row].astype(F32), axis=0, keepdims=True)


def back_call(dq, dk, dv, pre, x, wq, w_in, gains):
    tokens, width = dq.shape
    units, feats = w_in.shape
    part = pl.BlockSpec((TILE, width), lambda i: (i, 0))
    return pl.pallas_call(
        back_kernel,
        grid=(tokens // TILE,),
        in_specs=[
            part,
            part,
            part,
            pl.BlockSpec((TILE, units), lambda i: (i, 0)),
            pl.BlockSpec((TILE, feats), lambda i: (i, 0)),
            pl.BlockSpec((3 * width, feats), lambda i: (0, 0)),
            pl.BlockSpec((units, feats), lambda i: (0, 0)),
            pl.BlockSpec((2, feats), lambda i: (0, 0)),
        ],
        out_specs=[
            pl.BlockSpec((TILE, feats), lambda i: (i, 0)),
            pl.BlockSpec((4, feats), lambda i: (0, 0)),
            pl.BlockSpec((1, 3 * width), lambda i: (0, 0)),
        ],
        out_shape=[
            jax.ShapeDtypeStruct((tokens, feats), BF),
            jax.ShapeDtypeStruct((4, feats), F32),
            jax.ShapeDtypeStruct((1, 3 * width), F32),
        ],
        compiler_params=params("arbitrary"),
        cost_estimate=cost(
            2 * tokens * feats * (3 * width + units),
            2 * (tokens * (3 * width + units + 2 * feats) + feats * (3 * width + units)),
        ),
        name="back",
    )(dq, dk, dv, pre, x, wq, w_in, gains)


def body(
    hidden_in,
    segment_ids,
    norm_gains,
    norm_biases,
    qkv_weight,
    qkv_bias,
    dense_weight,
    fc_in_weight,
    fc_in_bias,
    fc_out_weight,
    out_biases,
    out_grad,
):
    chips = lax.axis_size("tensor")
    rows_of_chips = lax.axis_size("fsdp")
    tensor_index = lax.axis_index("tensor")
    core = lax.axis_index("ctx")
    local_seqs, span, feats = hidden_in.shape
    sharing = chips // local_seqs
    ranks = 2 * sharing
    tokens = 2 * chips * span
    tiles = tokens // TILE
    local_heads = qkv_bias.shape[0]
    local_units = fc_in_bias.shape[0]
    cols = qkv_weight.shape[0]
    own_seq = tensor_index // sharing
    rank = (tensor_index % sharing) * 2 + core
    swap = sharing == 1 and local_heads % 2 == 0
    heads = chips * local_heads // ranks
    units = chips * local_units // ranks
    gains = norm_gains.astype(F32)
    shifts = norm_biases.astype(F32)
    other_core = [(0, 1), (1, 0)]

    def both_cores(own, axis):
        far = lax.ppermute(own, "ctx", other_core)
        return jnp.where(
            core == 0, jnp.stack([own, far], axis=axis), jnp.stack([far, own], axis=axis)
        )

    def to_sequence(rows):
        if sharing > 1:
            rows = jnp.repeat(rows, sharing, axis=0)
        own = lax.all_to_all(rows, "tensor", 0, 0, tiled=True)
        return own, both_cores(own, 1).reshape(tokens, feats)

    def from_sequence(rows):
        rows = lax.all_to_all(rows, "tensor", 0, 0, tiled=True)
        if sharing > 1:
            rows = rows.reshape(local_seqs, sharing, span, feats).astype(F32)
            rows = jnp.sum(rows, axis=1).astype(BF)
        return rows

    def fold_cores(part):
        blocks = part.reshape(chips, 2, span, feats)
        own = lax.dynamic_index_in_dim(blocks, core, 1, keepdims=False)
        far = lax.dynamic_index_in_dim(blocks, 1 - core, 1, keepdims=False)
        return own.astype(F32) + lax.ppermute(far, "ctx", other_core).astype(F32)

    def gather_rows(shard):
        pieces, rows, _ = shard.shape
        if swap:
            mine = lax.all_to_all(shard, "ctx", 0, 0, tiled=False)
            mine = mine.transpose(1, 0, 2).reshape(rows, 2 * cols)
            full = lax.all_gather(mine, CHIPS, axis=0, tiled=False)
            full = full.reshape(rows_of_chips, chips, rows, 2 * cols)
            return full.transpose(1, 2, 0, 3).reshape(chips, rows, feats)
        full = lax.all_gather(shard.reshape(pieces * rows, cols), EVERY, axis=0, tiled=False)
        full = full.reshape(rows_of_chips, chips, 2, pieces, rows, cols)
        full = full.transpose(1, 3, 4, 0, 2, 5).reshape(chips * pieces, rows, feats)
        count = chips * pieces // ranks
        return lax.dynamic_slice_in_dim(full, rank * count, count, 0)

    def scatter_rows(full, pieces):
        count, rows, _ = full.shape
        full = full.astype(BF)
        if swap:
            full = full.reshape(chips, rows, rows_of_chips, 2 * cols).transpose(2, 0, 1, 3)
            full = full.reshape(rows_of_chips * chips, rows, 2 * cols)
            mine = lax.psum_scatter(full, CHIPS, scatter_dimension=0, tiled=True)
            mine = mine.reshape(rows, 2, cols).transpose(1, 0, 2)
            return lax.all_to_all(mine, "ctx", 0, 0, tiled=False).astype(F32)
        wide = jnp.zeros((chips * pieces, rows, feats), BF)
        wide = lax.dynamic_update_slice_in_dim(wide, full, rank * count, 0)
        wide = wide.reshape(chips, pieces, rows, rows_of_chips, 2, cols)
        wide = wide.transpose(3, 0, 4, 1, 2, 5).reshape(-1, pieces * rows, cols)
        mine = lax.psum_scatter(wide, EVERY, scatter_dimension=0, tiled=True)
        return mine.reshape(pieces, rows, cols).astype(F32)

    def own_pieces(full):
        pieces = full.shape[1]
        if swap:
            return lax.dynamic_index_in_dim(full, core, 1, keepdims=False)
        full = full.reshape((chips * pieces,) + full.shape[2:])
        count = chips * pieces // ranks
        return lax.dynamic_slice_in_dim(full, rank * count, count, 0)

    def place_pieces(part, pieces):
        size = part.shape[1]
        if swap:
            wide = jnp.zeros((chips, pieces, size), F32)
            return lax.dynamic_update_slice_in_dim(wide, part[:, None], core, 1)
        wide = jnp.zeros((chips * pieces, size), F32)
        wide = lax.dynamic_update_slice_in_dim(wide, part, rank * part.shape[0], 0)
        return wide.reshape(chips, pieces, size)

    unit_pieces = 2 if swap else local_heads
    unit_rows = local_units // unit_pieces
    head_pieces = 2 if swap else local_heads
    head_rows = local_heads // head_pieces

    own_x, x = to_sequence(hidden_in)
    own_dy, dy = to_sequence(out_grad)
    bias_vector = jnp.concatenate([qkv_bias.reshape(-1), fc_in_bias]).astype(F32)
    bias_all = lax.all_gather(bias_vector, "tensor", axis=0, tiled=False)
    qkv_shift = own_pieces(
        bias_all[:, : local_heads * 3 * HD].reshape(chips, head_pieces, head_rows * 3 * HD)
    )
    qkv_shift = qkv_shift.reshape(heads, 3, HD).transpose(1, 0, 2).reshape(1, -1)
    unit_shift = own_pieces(
        bias_all[:, local_heads * 3 * HD :].reshape(chips, unit_pieces, unit_rows)
    ).reshape(1, units)

    w_in = gather_rows(fc_in_weight.T.reshape(unit_pieces, unit_rows, cols))
    w_in = w_in.reshape(units, feats)
    w_out = gather_rows(fc_out_weight.reshape(unit_pieces, unit_rows, cols))
    w_out = w_out.reshape(units, feats)
    w_qkv = gather_rows(
        qkv_weight.transpose(1, 2, 0).reshape(head_pieces, head_rows * 3 * HD, cols)
    )
    w_qkv = w_qkv.reshape(heads, 3, HD, feats).transpose(1, 0, 2, 3).reshape(heads * 3 * HD, feats)
    w_dense = gather_rows(dense_weight.reshape(head_pieces, head_rows * HD, cols))
    w_dense = w_dense.reshape(heads * HD, feats)

    segments = lax.dynamic_index_in_dim(segment_ids, own_seq, 0, keepdims=False)
    places = lax.broadcasted_iota(jnp.int32, (tokens,), 0)
    change = jnp.concatenate(
        [jnp.ones((1,), jnp.int32), (segments[1:] != segments[:-1]).astype(jnp.int32)]
    )
    starts = lax.cummax(places * change, axis=0)
    begin = starts[::TILE] // TILE
    freqs = 10000.0 ** (-jnp.arange(0, ROT, 2, dtype=F32) / ROT)
    angle = (places - starts).astype(F32)[:, None] * freqs
    cos_own, sin_own = jnp.cos(angle), jnp.sin(angle)
    rest = jnp.zeros((tokens, HD - ROT), F32)
    cos_lanes = jnp.concatenate([cos_own, cos_own, rest + 1.0] * 2, axis=1)
    sin_lanes = jnp.concatenate([-sin_own, sin_own, rest] * 2, axis=1)
    cos_rows = cos_own.reshape(tiles, TILE, ROT // 2).transpose(0, 2, 1)
    sin_rows = sin_own.reshape(tiles, TILE, ROT // 2).transpose(0, 2, 1)

    one, two = norms_call(x, gains, shifts)
    active, grad_pre, unit_sum = units_call(two, dy, w_in, w_out, unit_shift)
    grad_w_in = tn(grad_pre, two)
    grad_w_out = tn(active, dy)
    grad_w_in = scatter_rows(grad_w_in.reshape(-1, unit_rows, feats), unit_pieces)
    grad_w_out = scatter_rows(grad_w_out.reshape(-1, unit_rows, feats), unit_pieces)

    qkv = qkv_call(one, w_qkv, qkv_shift, cos_lanes, sin_lanes)
    grad_att = nt(dy, w_dense).astype(BF)
    attended, dq, dk, dv = attend_call(
        begin, qkv, grad_att, starts.reshape(tiles, 1, TILE), cos_rows, sin_rows
    )
    grad_w_dense = scatter_rows(
        tn(attended, dy).reshape(-1, head_rows * HD, feats), head_pieces
    )

    part = fold_cores(output_call(attended, active, w_dense, w_out))
    bias_rows = out_biases.astype(F32)
    wide_x = own_x.astype(F32)
    residual = wide_x + bias_rows[0] + bias_rows[1]
    upstream = own_dy.astype(F32)
    if sharing > 1:
        leader = tensor_index % sharing == 0
        residual = jnp.where(leader, residual, 0.0)
        upstream = jnp.where(leader, upstream, 0.0)
    hidden_out = from_sequence((residual + part).astype(BF))

    back, stats, qkv_sum = back_call(dq, dk, dv, grad_pre, x, w_qkv, w_in, gains)
    grad_w_qkv = jnp.stack([tn(g, one).astype(BF) for g in (dq, dk, dv)])
    grad_w_qkv = grad_w_qkv.reshape(3, heads, HD, feats).transpose(1, 0, 2, 3)
    grad_w_qkv = scatter_rows(grad_w_qkv.reshape(-1, head_rows * 3 * HD, feats), head_pieces)

    e = fold_cores(back)
    normed, inverse = layer_stats(wide_x)
    through = inverse * (
        e
        - jnp.mean(e, axis=-1, keepdims=True)
        - normed * jnp.mean(e * normed, axis=-1, keepdims=True)
    )
    input_grad = from_sequence((upstream + through).astype(BF))

    qkv_sum = qkv_sum.reshape(3, heads, HD).transpose(1, 0, 2).reshape(-1, head_rows * 3 * HD)
    qkv_sum = place_pieces(qkv_sum, head_pieces)
    unit_sum = place_pieces(unit_sum.reshape(-1, unit_rows), unit_pieces)
    out_sum = jnp.sum(out_grad.astype(F32), axis=(0, 1))
    packed = jnp.concatenate(
        [stats.reshape(-1), out_sum, qkv_sum.reshape(-1), unit_sum.reshape(-1)]
    )
    packed = lax.psum(packed, EVERY)
    sums = packed[: 5 * feats].reshape(5, feats)
    qkv_size = chips * local_heads * 3 * HD
    qkv_all = packed[5 * feats : 5 * feats + qkv_size].reshape(chips, local_heads, 3 * HD)
    unit_all = packed[5 * feats + qkv_size :].reshape(chips, local_units)
    grad_qkv_b = lax.dynamic_index_in_dim(qkv_all, tensor_index, 0, keepdims=False)
    grad_unit_b = lax.dynamic_index_in_dim(unit_all, tensor_index, 0, keepdims=False)
    return (
        hidden_out,
        input_grad,
        sums[0:2],
        sums[2:4],
        grad_w_qkv.reshape(local_heads, 3 * HD, cols).transpose(2, 0, 1),
        grad_qkv_b,
        grad_w_dense.reshape(local_heads, HD, cols),
        grad_w_in.reshape(local_units, cols).T,
        grad_unit_b,
        grad_w_out.reshape(local_units, cols),
        jnp.stack([sums[4], sums[4]]),
    )


def solution(mesh):
    rows = P("fsdp", ("tensor", "ctx"), None)
    weights = (
        P(("fsdp", "ctx"), "tensor", None),
        P("tensor", None),
        P("tensor", None, ("fsdp", "ctx")),
        P(("fsdp", "ctx"), "tensor"),
        P("tensor"),
        P("tensor", ("fsdp", "ctx")),
    )
    return jax.shard_map(
        body,
        mesh=mesh,
        in_specs=(rows, P("fsdp", None), P(), P()) + weights + (P(), rows),
        out_specs=(rows, rows, P(), P()) + weights + (P(),),
        check_vma=False,
    )
```

```python
import jax
import jax.numpy as jnp
from jax import lax
from jax.experimental import pallas as pl
from jax.experimental.layout import Layout, with_layout_constraint
from jax.experimental.pallas import tpu as pltpu
from jax.sharding import PartitionSpec as P

HD = 64
ROT = 16
PAIR = 2 * HD
TILE = 256
WIDE = 512
SPAN = 1024
CHIPS = ("fsdp", "tensor")
EVERY = ("fsdp", "tensor", "ctx")
BF = jnp.bfloat16
F32 = jnp.float32
epsilon = 1e-05
VMEM = 56 * 1024 * 1024


AFTER = pl.BlockSpec(memory_space=pl.ANY)


def nt(a, b):
    return lax.dot_general(a, b, (((1,), (1,)), ((), ())), preferred_element_type=F32)


def nn(a, b):
    return jnp.dot(a, b, preferred_element_type=F32)


def tn(a, b):
    return lax.dot_general(a, b, (((0,), (0,)), ((), ())), preferred_element_type=F32)


def params(*kinds):
    return pltpu.CompilerParams(dimension_semantics=kinds, vmem_limit_bytes=VMEM)


def cost(flops, moved, special=0):
    return pl.CostEstimate(flops=int(flops), bytes_accessed=int(moved), transcendentals=int(special))


def layer_stats(values):
    center = values - jnp.mean(values, axis=-1, keepdims=True)
    inverse = lax.rsqrt(jnp.mean(center * center, axis=-1, keepdims=True) + epsilon)
    return (center * inverse, inverse)


def in_order(core_ref, own_ref, far_ref):
    first = core_ref[0] == 0
    own, far = own_ref[0], far_ref[0]
    return jnp.where(first, own, far), jnp.where(first, far, own)


def merge_kernel(core_ref, own_ref, far_ref, after_ref, out_ref):
    span = own_ref.shape[1]
    low, high = in_order(core_ref, own_ref, far_ref)
    out_ref[:span, :] = low
    out_ref[span:, :] = high


def norms_kernel(core_ref, own_ref, far_ref, gain_ref, shift_ref, out_ref, one_ref, two_ref):
    span = own_ref.shape[1]
    for index, rows in enumerate(in_order(core_ref, own_ref, far_ref)):
        place = slice(index * span, (index + 1) * span)
        out_ref[place, :] = rows
        normed, _ = layer_stats(rows.astype(F32))
        one_ref[place, :] = (normed * gain_ref[0:1, :] + shift_ref[0:1, :]).astype(BF)
        two_ref[place, :] = (normed * gain_ref[1:2, :] + shift_ref[1:2, :]).astype(BF)


def merge_call(core, own, far, after=None, gains=None, shifts=None):
    blocks, span, feats = own.shape
    tokens = 2 * blocks * span
    block = pl.BlockSpec((1, span, feats), lambda i, *_: (i, 0, 0))
    row = pl.BlockSpec((2 * span, feats), lambda i, *_: (i, 0))
    pair = pl.BlockSpec((2, feats), lambda i, *_: (0, 0))
    plain = gains is None
    count = 1 if plain else 3
    return pl.pallas_call(
        merge_kernel if plain else norms_kernel,
        grid_spec=pltpu.PrefetchScalarGridSpec(
            num_scalar_prefetch=1,
            grid=(blocks,),
            in_specs=[block, block] + ([AFTER] if plain else [pair, pair]),
            out_specs=[row] * count,
        ),
        out_shape=[jax.ShapeDtypeStruct((tokens, feats), BF)] * count,
        compiler_params=params("arbitrary"),
        cost_estimate=cost(tokens * feats * 12, tokens * feats * 2 * (1 + count)),
        name="merge" if plain else "norms",
    )(*((core, own, far) + ((after,) if plain else (gains, shifts))))


def block_of(ref, side, first, count):
    rows = ref[side, :, first : first + count, :]
    return rows.reshape(-1, rows.shape[-1])


def columns(side, wide):
    return slice(side * wide, (side + 1) * wide)


def qkv_kernel(one_ref, dy_ref, w_ref, bias_ref, cos_ref, sin_ref, after_ref, out_ref, grad_ref):
    sides, groups, _, wide = w_ref.shape
    width = groups * HD
    lane = lax.broadcasted_iota(jnp.int32, (WIDE, PAIR), 1) % HD
    low_half = lane < ROT // 2
    cosine = cos_ref[...]
    sine_part = sin_ref[...]

    def product(rows_ref, part):
        return sum(
            nt(rows_ref[:, columns(f, wide)], block_of(w_ref, f, part * HD, HD))
            for f in range(sides)
        )

    for part in range(3):
        span = slice(part * width, (part + 1) * width)
        whole = product(one_ref, part) + bias_ref[:, span]
        if part == 2:
            out_ref[:, span] = whole.astype(BF)
            continue
        for first in range(0, width, PAIR):
            u = whole[:, first : first + PAIR]
            turned = jnp.where(
                low_half, pltpu.roll(u, PAIR - ROT // 2, 1), pltpu.roll(u, ROT // 2, 1)
            )
            u = u * cosine + turned * sine_part
            if part == 0:
                u = u * HD ** (-0.5)
            out_ref[:, part * width + first : part * width + first + PAIR] = u.astype(BF)
    grad_ref[...] = product(dy_ref, 3).astype(BF)


def qkv_call(one, dy, w, bias, cosine, sine_part, after):
    tokens, feats = one.shape
    width = w.shape[1] * HD
    row = lambda size: pl.BlockSpec((WIDE, size), lambda i: (i, 0))
    return pl.pallas_call(
        qkv_kernel,
        grid=(tokens // WIDE,),
        in_specs=[
            row(feats),
            row(feats),
            pl.BlockSpec(w.shape, lambda i: (0, 0, 0, 0)),
            pl.BlockSpec((1, 3 * width), lambda i: (0, 0)),
            row(PAIR),
            row(PAIR),
            AFTER,
        ],
        out_specs=[row(3 * width), row(width)],
        out_shape=[
            jax.ShapeDtypeStruct((tokens, 3 * width), BF),
            jax.ShapeDtypeStruct((tokens, width), BF),
        ],
        compiler_params=params("arbitrary"),
        cost_estimate=cost(16 * tokens * feats * width, 8 * tokens * (feats + width)),
        name="qkv",
    )(one, dy, w, bias, cosine, sine_part, after)


def turn_back(g, cosine, sine_part):
    eight = ROT // 2
    parts = []
    for head in range(2):
        own = g[head * HD : (head + 1) * HD]
        low, high = own[:eight], own[eight:ROT]
        parts += [low * cosine + high * sine_part, high * cosine - low * sine_part, own[ROT:]]
    return jnp.concatenate(parts, axis=0)


def attend_kernel(
    begin_ref,
    q_ref,
    k_ref,
    v_ref,
    grad_ref,
    doc_ref,
    cos_ref,
    sin_ref,
    att_ref,
    dq_ref,
    dk_ref,
    dv_ref,
    score_ref,
    prob_ref,
    key_turn_ref,
    value_turn_ref,
    dk_sum_ref,
    dv_sum_ref,
):
    tile = pl.program_id(1)
    tiles = pl.num_programs(1)
    total_tiles = k_ref.shape[0] // TILE

    @pl.when(tile == 0)
    def _():
        dk_sum_ref[...] = jnp.zeros_like(dk_sum_ref)
        dv_sum_ref[...] = jnp.zeros_like(dv_sum_ref)

        def turn(block, _):
            rows = pl.ds(pl.multiple_of(block * TILE, TILE), TILE)
            key_turn_ref[block] = k_ref[rows, :].astype(F32).T.astype(BF)
            value_turn_ref[block] = v_ref[rows, :].astype(F32).T.astype(BF)
            return 0

        lax.fori_loop(0, total_tiles, turn, 0)

    lane = lax.broadcasted_iota(jnp.int32, (TILE, PAIR), 1)
    q_wide = q_ref[...].astype(F32)
    g_wide = grad_ref[...].astype(F32)
    q_heads = [
        jnp.where(lane < HD, q_wide, 0.0).astype(BF),
        jnp.where(lane >= HD, q_wide, 0.0).astype(BF),
    ]
    g_heads = [
        jnp.where(lane < HD, g_wide, 0.0).astype(BF),
        jnp.where(lane >= HD, g_wide, 0.0).astype(BF),
    ]
    first = begin_ref[tile]
    doc = doc_ref[0]
    key_place = lax.broadcasted_iota(jnp.int32, (TILE, TILE), 0)
    query_place = lax.broadcasted_iota(jnp.int32, (TILE, TILE), 1) + tile * TILE

    def rows_of(block):
        return pl.ds(pl.multiple_of(block * TILE, TILE), TILE)

    def scores_step(block, tops):
        keys = k_ref[rows_of(block), :]
        place = key_place + block * TILE
        allowed = (place >= doc) & (place <= query_place)
        new = []
        for head in range(2):
            s = jnp.where(allowed, nt(keys, q_heads[head]), -1e30)
            score_ref[head, rows_of(block - first), :] = s
            new.append(jnp.maximum(tops[head], jnp.max(s, axis=0, keepdims=True)))
        return tuple(new)

    lowest = jnp.full((1, TILE), -1e30, F32)
    tops = lax.fori_loop(first, tile + 1, scores_step, (lowest, lowest))

    def exp_step(block, sums):
        values = v_ref[rows_of(block), :]
        new = []
        for head in range(2):
            e = jnp.exp(score_ref[head, rows_of(block - first), :] - tops[head])
            score_ref[head, rows_of(block - first), :] = e
            gp = nt(values, g_heads[head])
            prob_ref[head, rows_of(block - first), :] = gp
            new.append(sums[2 * head] + jnp.sum(e, axis=0, keepdims=True))
            new.append(sums[2 * head + 1] + jnp.sum(e * gp, axis=0, keepdims=True))
        return tuple(new)

    none = jnp.zeros((1, TILE), F32)
    sums = lax.fori_loop(first, tile + 1, exp_step, (none,) * 4)
    inverse = [1.0 / sums[0], 1.0 / sums[2]]
    means = [sums[1] * inverse[0], sums[3] * inverse[1]]

    def grad_step(block, turned):
        new = []
        dk = dk_sum_ref[rows_of(block), :]
        dv = dv_sum_ref[rows_of(block), :]
        for head in range(2):
            p = score_ref[head, rows_of(block - first), :] * inverse[head]
            gs = (p * (prob_ref[head, rows_of(block - first), :] - means[head])).astype(BF)
            p_low = p.astype(BF)
            dv = dv + nn(p_low, g_heads[head])
            dk = dk + nn(gs, q_heads[head])
            half = slice(head * HD, (head + 1) * HD)
            new.append(turned[2 * head] + nn(value_turn_ref[block, half, :], p_low))
            new.append(turned[2 * head + 1] + nn(key_turn_ref[block, half, :], gs))
        dk_sum_ref[rows_of(block), :] = dk
        dv_sum_ref[rows_of(block), :] = dv
        return tuple(new)

    flat = jnp.zeros((HD, TILE), F32)
    turned = lax.fori_loop(first, tile + 1, grad_step, (flat,) * 4)
    att_ref[...] = jnp.concatenate([turned[0], turned[2]], axis=0).T.astype(BF)
    dq = jnp.concatenate([turned[1], turned[3]], axis=0) * HD ** (-0.5)
    dq_ref[...] = turn_back(dq, cos_ref[tile], sin_ref[tile]).T.astype(BF)

    @pl.when(tile == tiles - 1)
    def _():
        dv_ref[...] = dv_sum_ref[...].astype(BF)

        def finish(block, _):
            g = dk_sum_ref[rows_of(block), :].T
            dk_ref[rows_of(block), :] = turn_back(g, cos_ref[block], sin_ref[block]).T.astype(BF)
            return 0

        lax.fori_loop(0, total_tiles, finish, 0)


def attend_call(begin, qkv, grad_att, doc, cosine, sine_part):
    tokens = qkv.shape[0]
    width = qkv.shape[1] // 3
    pairs = width // PAIR
    tiles = tokens // TILE
    reach = SPAN + TILE
    query = pl.BlockSpec((TILE, PAIR), lambda p, i, *_: (i, p))
    whole = pl.BlockSpec((tokens, PAIR), lambda p, i, *_: (0, p))
    table = pl.BlockSpec((tiles, ROT // 2, TILE), lambda p, i, *_: (0, 0, 0))
    return pl.pallas_call(
        attend_kernel,
        grid_spec=pltpu.PrefetchScalarGridSpec(
            num_scalar_prefetch=1,
            grid=(pairs, tiles),
            in_specs=[
                query,
                pl.BlockSpec((tokens, PAIR), lambda p, i, *_: (0, pairs + p)),
                pl.BlockSpec((tokens, PAIR), lambda p, i, *_: (0, 2 * pairs + p)),
                query,
                pl.BlockSpec((1, 1, TILE), lambda p, i, *_: (i, 0, 0)),
                table,
                table,
            ],
            out_specs=[query, query, whole, whole],
            scratch_shapes=[
                pltpu.VMEM((2, reach, TILE), F32),
                pltpu.VMEM((2, reach, TILE), F32),
                pltpu.VMEM((tiles, PAIR, TILE), BF),
                pltpu.VMEM((tiles, PAIR, TILE), BF),
                pltpu.VMEM((tokens, PAIR), F32),
                pltpu.VMEM((tokens, PAIR), F32),
            ],
        ),
        out_shape=[jax.ShapeDtypeStruct((tokens, width), BF)] * 4,
        compiler_params=params("arbitrary", "arbitrary"),
        cost_estimate=cost(
            tokens * 800 * width * 4 * 12, tokens * width * 16, tokens * 600 * (width // HD)
        ),
        name="attend",
    )(begin, qkv, qkv, qkv, grad_att, doc, cosine, sine_part)


def normal(v):
    bell = jnp.exp(-0.5 * v * v)
    t = 1.0 / (1.0 + 0.2316418882 * jnp.abs(v))
    tail = 0.7107068705 + t * (-0.7265760135 + t * 0.5307027145)
    tail = 0.127414796 + t * (-0.142248368 + t * tail)
    tail = jnp.where(v < 0, 1.0, -1.0) * (t * tail * bell)
    return jnp.where(v < 0, 0.0, 1.0) + tail, bell * 0.3989422804014327


def units_kernel(two_ref, dy_ref, win_ref, wout_ref, bias_ref, act_ref, pre_ref, sum_ref):
    sides, _, rows, wide = win_ref.shape
    pre = bias_ref[...]
    upstream = 0.0
    for f in range(sides):
        pre = pre + nt(two_ref[:, columns(f, wide)], block_of(win_ref, f, 0, rows))
        upstream = upstream + nt(dy_ref[:, columns(f, wide)], block_of(wout_ref, f, 0, rows))
    cdf, density = normal(pre)
    act_ref[...] = (pre * cdf).astype(BF)
    back = (upstream * (cdf + pre * density)).astype(BF)
    pre_ref[...] = back

    @pl.when(pl.program_id(1) == 0)
    def _():
        sum_ref[...] = jnp.zeros_like(sum_ref)

    sum_ref[...] += jnp.sum(back.astype(F32), axis=0, keepdims=True)


def units_call(two, dy, w, bias, rows):
    tokens, feats = two.shape
    sides, groups, _, wide = w.shape
    units = groups * rows
    taken = max(1, 512 // rows)
    step = taken * rows
    row = pl.BlockSpec((WIDE, feats), lambda j, i: (i, 0))
    line = pl.BlockSpec((1, step), lambda j, i: (0, j))
    out = pl.BlockSpec((WIDE, step), lambda j, i: (i, j))
    return pl.pallas_call(
        units_kernel,
        grid=(units // step, tokens // WIDE),
        in_specs=[
            row,
            row,
            pl.BlockSpec((sides, taken, rows, wide), lambda j, i: (0, j, 0, 0)),
            pl.BlockSpec((sides, taken, rows, wide), lambda j, i: (0, j, 1, 0)),
            line,
        ],
        out_specs=[out, out, line],
        out_shape=[
            jax.ShapeDtypeStruct((tokens, units), BF),
            jax.ShapeDtypeStruct((tokens, units), BF),
            jax.ShapeDtypeStruct((1, units), F32),
        ],
        compiler_params=params("arbitrary", "arbitrary"),
        cost_estimate=cost(10 * tokens * feats * units, 40 * tokens * feats, 2 * tokens * units),
        name="units",
    )(two, dy, w, w, bias)


def unit_grads_kernel(pre_ref, two_ref, act_ref, dy_ref, out_ref):
    _, taken, rows, wide = out_ref.shape
    rows = rows // 2
    got = tn(pre_ref[...], two_ref[...]).astype(BF)
    out_ref[0, :, :rows, :] = got.reshape(taken, rows, wide)
    got = tn(act_ref[...], dy_ref[...]).astype(BF)
    out_ref[0, :, rows:, :] = got.reshape(taken, rows, wide)


def unit_grads_call(pre, two, act, dy, sides, groups):
    tokens, feats = two.shape
    units = act.shape[1]
    rows, wide = units // groups, feats // sides
    taken = max(1, 512 // rows)
    left = pl.BlockSpec((tokens, taken * rows), lambda f, t: (0, t))
    right = pl.BlockSpec((tokens, wide), lambda f, t: (0, f))
    return pl.pallas_call(
        unit_grads_kernel,
        grid=(sides, groups // taken),
        in_specs=[left, right, left, right],
        out_specs=pl.BlockSpec((1, taken, 2 * rows, wide), lambda f, t: (f, t, 0, 0)),
        out_shape=jax.ShapeDtypeStruct((sides, groups, 2 * rows, wide), BF),
        compiler_params=params("arbitrary", "arbitrary"),
        cost_estimate=cost(6 * tokens * feats * units, 4 * tokens * (feats + 2 * units)),
        name="unit_grads",
    )(pre, two, act, dy)


def head_grads_kernel(dq_ref, dk_ref, dv_ref, att_ref, one_ref, dy_ref, after_ref, out_ref):
    groups, _, wide = out_ref.shape[1:]
    pairs = ((dq_ref, one_ref), (dk_ref, one_ref), (dv_ref, one_ref), (att_ref, dy_ref))
    for part, (left, right) in enumerate(pairs):
        got = tn(left[...], right[...]).astype(BF)
        out_ref[0, :, part * HD : (part + 1) * HD, :] = got.reshape(groups, HD, wide)


def head_grads_call(dq, dk, dv, att, one, dy, sides, after):
    tokens, feats = one.shape
    width = dq.shape[1]
    groups, wide = width // HD, feats // sides
    left = pl.BlockSpec((tokens, width), lambda f: (0, 0))
    right = pl.BlockSpec((tokens, wide), lambda f: (0, f))
    return pl.pallas_call(
        head_grads_kernel,
        grid=(sides,),
        in_specs=[left] * 4 + [right] * 2 + [AFTER],
        out_specs=pl.BlockSpec((1, groups, 4 * HD, wide), lambda f: (f, 0, 0, 0)),
        out_shape=jax.ShapeDtypeStruct((sides, groups, 4 * HD, wide), BF),
        compiler_params=params("arbitrary"),
        cost_estimate=cost(12 * tokens * feats * width, 4 * tokens * (feats + 2 * width)),
        name="head_grads",
    )(dq, dk, dv, att, one, dy, after)


def keep_and_send(core_ref, whole, keep_ref, send_ref, place):
    blocks, span, _ = keep_ref.shape
    first = core_ref[0] == 0
    for block in range(blocks):
        at = 2 * block * span
        low, high = whole[at : at + span], whole[at + span : at + 2 * span]
        keep_ref[block, :, place] = jnp.where(first, low, high)
        send_ref[block, :, place] = jnp.where(first, high, low).astype(BF)


def shared_specs(blocks, span, feats):
    block = pl.BlockSpec((WIDE // (2 * span), span, feats), lambda i, *_: (i, 0, 0))
    shape = (blocks, span, feats)
    return [block, block], [jax.ShapeDtypeStruct(shape, F32), jax.ShapeDtypeStruct(shape, BF)]


def output_kernel(core_ref, att_ref, act_ref, wd_ref, wout_ref, keep_ref, send_ref):
    sides, _, rows, wide = wout_ref.shape
    for f in range(sides):
        whole = nn(att_ref[...], block_of(wd_ref, f, 0, HD))
        whole += nn(act_ref[...], block_of(wout_ref, f, 0, rows))
        keep_and_send(core_ref, whole, keep_ref, send_ref, columns(f, wide))


def output_call(core, span, att, act, w_heads, w_units, rows):
    tokens, width = att.shape
    units = act.shape[1]
    sides, groups, _, wide = w_units.shape
    feats = sides * wide
    step = WIDE
    specs, shapes = shared_specs(tokens // (2 * span), span, feats)
    return pl.pallas_call(
        output_kernel,
        grid_spec=pltpu.PrefetchScalarGridSpec(
            num_scalar_prefetch=1,
            grid=(tokens // step,),
            in_specs=[
                pl.BlockSpec((step, width), lambda i, *_: (i, 0)),
                pl.BlockSpec((step, units), lambda i, *_: (i, 0)),
                pl.BlockSpec((sides, groups, HD, wide), lambda i, *_: (0, 0, 3, 0)),
                pl.BlockSpec((sides, groups, rows, wide), lambda i, *_: (0, 0, 1, 0)),
            ],
            out_specs=specs,
        ),
        out_shape=shapes,
        compiler_params=params("arbitrary"),
        cost_estimate=cost(
            3 * tokens * feats * (width + units),
            2 * (tokens * (width + units + 2 * feats) + feats * (width + units)),
        ),
        name="output",
    )(core, att, act, w_heads, w_units)


def back_kernel(
    core_ref,
    dq_ref,
    dk_ref,
    dv_ref,
    pre_ref,
    x_ref,
    w_ref,
    win_ref,
    gain_ref,
    after_ref,
    keep_ref,
    send_ref,
    stat_ref,
    bias_ref,
):
    width = dq_ref.shape[1]
    sides, _, rows, wide = win_ref.shape
    parts = [dq_ref[...], dk_ref[...], dv_ref[...]]
    normed, _ = layer_stats(x_ref[...].astype(F32))

    @pl.when(pl.program_id(0) == 0)
    def _():
        stat_ref[...] = jnp.zeros_like(stat_ref)
        bias_ref[...] = jnp.zeros_like(bias_ref)

    for f in range(sides):
        place = columns(f, wide)
        one = sum(nn(part, block_of(w_ref, f, at * HD, HD)) for at, part in enumerate(parts))
        two = nn(pre_ref[...], block_of(win_ref, f, 0, rows))
        whole = one * gain_ref[0:1, place] + two * gain_ref[1:2, place]
        keep_and_send(core_ref, whole, keep_ref, send_ref, place)
        n = normed[:, place]
        for row, value in enumerate((one * n, two * n, one, two)):
            stat_ref[row : row + 1, place] += jnp.sum(value, axis=0, keepdims=True)
    for row in range(3):
        span = slice(row * width, (row + 1) * width)
        bias_ref[:, span] += jnp.sum(parts[row].astype(F32), axis=0, keepdims=True)


def back_call(core, span, dq, dk, dv, pre, x, w_heads, w_units, gains, rows, after):
    tokens, width = dq.shape
    units = pre.shape[1]
    sides, groups, _, wide = w_units.shape
    feats = sides * wide
    step = WIDE
    part = pl.BlockSpec((step, width), lambda i, *_: (i, 0))
    specs, shapes = shared_specs(tokens // (2 * span), span, feats)
    return pl.pallas_call(
        back_kernel,
        grid_spec=pltpu.PrefetchScalarGridSpec(
            num_scalar_prefetch=1,
            grid=(tokens // step,),
            in_specs=[
                part,
                part,
                part,
                pl.BlockSpec((step, units), lambda i, *_: (i, 0)),
                pl.BlockSpec((step, feats), lambda i, *_: (i, 0)),
                pl.BlockSpec(w_heads.shape, lambda i, *_: (0, 0, 0, 0)),
                pl.BlockSpec((sides, groups, rows, wide), lambda i, *_: (0, 0, 0, 0)),
                pl.BlockSpec((2, feats), lambda i, *_: (0, 0)),
                AFTER,
            ],
            out_specs=specs
            + [
                pl.BlockSpec((4, feats), lambda i, *_: (0, 0)),
                pl.BlockSpec((1, 3 * width), lambda i, *_: (0, 0)),
            ],
        ),
        out_shape=shapes
        + [
            jax.ShapeDtypeStruct((4, feats), F32),
            jax.ShapeDtypeStruct((1, 3 * width), F32),
        ],
        compiler_params=params("arbitrary"),
        cost_estimate=cost(
            3 * tokens * feats * (3 * width + units),
            2 * (tokens * (3 * width + units + 3 * feats) + feats * (3 * width + units)),
        ),
        name="back",
    )(core, dq, dk, dv, pre, x, w_heads, w_units, gains, after)


def fold_kernel(side_ref, own_ref, far_ref, after_ref, out_ref):
    out_ref[...] = (own_ref[0].astype(F32) + far_ref[...].astype(F32)).astype(BF)


def fold_call(side, full, far, after):
    groups, rows, wide = far.shape
    block = pl.BlockSpec((1, rows, wide), lambda i, *_: (i, 0, 0))
    return pl.pallas_call(
        fold_kernel,
        grid_spec=pltpu.PrefetchScalarGridSpec(
            num_scalar_prefetch=1,
            grid=(groups,),
            in_specs=[
                pl.BlockSpec((1, 1, rows, wide), lambda i, side_ref: (side_ref[0], i, 0, 0)),
                block,
                AFTER,
            ],
            out_specs=block,
        ),
        out_shape=jax.ShapeDtypeStruct(far.shape, BF),
        compiler_params=params("arbitrary"),
        cost_estimate=cost(far.size * 2, far.size * 6),
        name="fold",
    )(side, full, far, after)


def finish_kernel(keep_ref, far_ref, x_ref, dy_ref, after_ref, out_ref):
    e = keep_ref[0] + far_ref[0].astype(F32)
    normed, inverse = layer_stats(x_ref[0].astype(F32))
    through = inverse * (
        e
        - jnp.mean(e, axis=-1, keepdims=True)
        - normed * jnp.mean(e * normed, axis=-1, keepdims=True)
    )
    out_ref[0] = (dy_ref[0].astype(F32) + through).astype(BF)


def finish_call(keep, far, x, dy, after):
    block = pl.BlockSpec((1,) + keep.shape[1:], lambda i: (i, 0, 0))
    return pl.pallas_call(
        finish_kernel,
        grid=(keep.shape[0],),
        in_specs=[block] * 4 + [AFTER],
        out_specs=block,
        out_shape=jax.ShapeDtypeStruct(keep.shape, BF),
        compiler_params=params("arbitrary"),
        cost_estimate=cost(keep.size * 20, keep.size * 12),
        name="finish",
    )(keep, far, x, dy, after)


def swap_cores(v):
    return lax.ppermute(v, "ctx", [(0, 1), (1, 0)])


def body(
    hidden_in,
    segment_ids,
    norm_gains,
    norm_biases,
    qkv_weight,
    qkv_bias,
    dense_weight,
    fc_in_weight,
    fc_in_bias,
    fc_out_weight,
    out_biases,
    out_grad,
):
    chips = lax.axis_size("tensor")
    rows_of_chips = lax.axis_size("fsdp")
    tensor_index = lax.axis_index("tensor")
    core = lax.axis_index("ctx")
    side = lax.axis_index("fsdp")
    local_seqs, span, feats = hidden_in.shape
    sharing = chips // local_seqs
    ranks = 2 * sharing
    tokens = 2 * chips * span
    tiles = tokens // TILE
    local_heads = qkv_bias.shape[0]
    local_units = fc_in_bias.shape[0]
    cols = qkv_weight.shape[0]
    own_seq = tensor_index // sharing
    rank = (tensor_index % sharing) * 2 + core
    swap = (
        sharing == 1 and local_heads == 2 and rows_of_chips == 2 and chips & (chips - 1) == 0
    )
    heads = chips * local_heads // ranks
    units = chips * local_units // ranks
    gains = norm_gains.astype(F32)
    shifts = norm_biases.astype(F32)
    core_scalar = core.reshape(1)

    def to_chip(rows):
        if sharing > 1:
            rows = jnp.repeat(rows, sharing, axis=0)
        return lax.all_to_all(rows, "tensor", 0, 0, tiled=True)

    def from_chip(rows):
        rows = lax.all_to_all(rows, "tensor", 0, 0, tiled=True)
        if sharing > 1:
            rows = rows.reshape(local_seqs, sharing, span, feats).astype(F32)
            rows = jnp.sum(rows, axis=1).astype(BF)
        return rows

    def ordered(own, far, axis):
        return jnp.where(
            core == 0,
            jnp.concatenate([own, far], axis=axis),
            jnp.concatenate([far, own], axis=axis),
        )

    def gather_rows(shard, extra=None):
        rows = shard.shape[1]
        if swap:
            own = lax.dynamic_index_in_dim(shard, core, 0, keepdims=False)
            far = lax.dynamic_index_in_dim(shard, 1 - core, 0, keepdims=False)
            mine = ordered(own, swap_cores(far), 1)
            if extra is not None:
                mine = jnp.concatenate([mine, extra])
            full = lax.all_gather(mine, CHIPS, axis=0, tiled=False)
            return full.reshape((rows_of_chips, chips) + mine.shape)
        full = lax.all_gather(shard.reshape(pieces * rows, cols), EVERY, axis=0, tiled=False)
        full = full.reshape(rows_of_chips, chips, 2, pieces, rows, cols)
        full = full.transpose(1, 3, 4, 0, 2, 5).reshape(1, chips * pieces, rows, feats)
        count = chips * pieces // ranks
        return lax.dynamic_slice_in_dim(full, rank * count, count, 1)

    def side_swap(v):
        return lax.ppermute(v, "fsdp", [(0, 1), (1, 0)])

    def sum_chips(full, axes):
        mine = lax.psum_scatter(full, axes, scatter_dimension=0, tiled=True)
        return with_layout_constraint(mine, Layout((0, 1, 2)))

    def to_cores(mine):
        mine = mine.reshape(-1, 2, cols)
        own = lax.dynamic_index_in_dim(mine, core, 1, keepdims=False)
        far = lax.dynamic_index_in_dim(mine, 1 - core, 1, keepdims=False)
        return ordered(own[None], swap_cores(far)[None], 0).astype(F32)

    def scatter_rows(full):
        rows = full.shape[2]
        wide = jnp.zeros((chips * pieces, rows, feats), BF)
        wide = lax.dynamic_update_slice_in_dim(wide, full[0], rank * full.shape[1], 0)
        wide = wide.reshape(chips, pieces, rows, rows_of_chips, 2, cols)
        wide = wide.transpose(3, 0, 4, 1, 2, 5).reshape(-1, pieces * rows, cols)
        mine = lax.psum_scatter(wide, EVERY, scatter_dimension=0, tiled=True)
        return mine.reshape(pieces, rows, cols).astype(F32)

    def own_pieces(full):
        full = full.reshape((chips * pieces,) + full.shape[2:])
        count = chips * pieces // ranks
        return lax.dynamic_slice_in_dim(full, rank * count, count, 0)

    def place_pieces(part):
        size = part.shape[1]
        if swap:
            wide = jnp.zeros((chips, pieces, size), F32)
            return lax.dynamic_update_slice_in_dim(wide, part[:, None], core, 1)
        wide = jnp.zeros((chips * pieces, size), F32)
        wide = lax.dynamic_update_slice_in_dim(wide, part, rank * part.shape[0], 0)
        return wide.reshape(chips, pieces, size)

    pieces = local_heads
    unit_rows = local_units // pieces
    unit_shards = jnp.concatenate(
        [
            fc_in_weight.T.reshape(pieces, unit_rows, cols),
            fc_out_weight.reshape(pieces, unit_rows, cols),
        ],
        axis=1,
    )
    head_shards = jnp.concatenate([qkv_weight.transpose(1, 2, 0), dense_weight], axis=1)

    own_x = to_chip(hidden_in)
    own_dy = to_chip(out_grad)
    if swap:
        shift_row = jnp.concatenate(
            [
                lax.dynamic_index_in_dim(qkv_bias, core, 0, keepdims=False),
                lax.dynamic_slice_in_dim(fc_in_bias, core * unit_rows, unit_rows, 0),
            ]
        )
        shift_rows = jnp.zeros((16, 2 * cols), BF)
        shift_rows = lax.dynamic_update_slice(shift_rows, shift_row[None], (0, 0))
        w_units = gather_rows(unit_shards, shift_rows)
        bias_all = w_units[0, :, 2 * unit_rows, :].astype(F32)
        w_heads = gather_rows(head_shards)
        qkv_shift = bias_all[:, : 3 * HD]
        unit_shift = bias_all[:, 3 * HD : 3 * HD + unit_rows]
    else:
        bias_vector = jnp.concatenate([qkv_bias.reshape(-1), fc_in_bias]).astype(F32)
        bias_all = lax.all_gather(bias_vector, "tensor", axis=0, tiled=False)
        qkv_size = local_heads * 3 * HD
        qkv_shift = own_pieces(bias_all[:, :qkv_size].reshape(chips, pieces, 3 * HD))
        unit_shift = own_pieces(bias_all[:, qkv_size:].reshape(chips, pieces, unit_rows))
        w_units = gather_rows(unit_shards)
        w_heads = gather_rows(head_shards)
    qkv_shift = qkv_shift.reshape(heads, 3, HD).transpose(1, 0, 2).reshape(1, -1)
    unit_shift = unit_shift.reshape(1, units)
    sides, groups = w_units.shape[:2]

    segments = lax.dynamic_index_in_dim(segment_ids, own_seq, 0, keepdims=False)
    places = lax.broadcasted_iota(jnp.int32, (tokens,), 0)
    change = jnp.concatenate(
        [jnp.ones((1,), jnp.int32), (segments[1:] != segments[:-1]).astype(jnp.int32)]
    )
    starts = lax.cummax(places * change, axis=0)
    begin = starts[::TILE] // TILE
    freqs = 10000.0 ** (-jnp.arange(0, ROT, 2, dtype=F32) / ROT)
    relative = (places - starts).astype(F32)[:, None]
    lane = jnp.arange(PAIR) % HD
    turning = lane < ROT
    lane_freqs = jnp.where(turning, freqs[lane % (ROT // 2)], 0.0)
    angle = relative * lane_freqs
    cos_lanes = jnp.cos(angle)
    sin_lanes = jnp.sin(angle) * jnp.where(lane < ROT // 2, -1.0, 1.0)
    cos_rows = cos_lanes[:, : ROT // 2].reshape(tiles, TILE, ROT // 2).transpose(0, 2, 1)
    sin_rows = -sin_lanes[:, : ROT // 2].reshape(tiles, TILE, ROT // 2).transpose(0, 2, 1)

    doc = starts.reshape(tiles, 1, TILE)
    x, one, two = merge_call(core_scalar, own_x, swap_cores(own_x), None, gains, shifts)
    (dy,) = merge_call(core_scalar, own_dy, swap_cores(own_dy), one)
    active, grad_pre, unit_sum = units_call(two, dy, w_units, unit_shift, unit_rows)
    unit_grads = unit_grads_call(grad_pre, two, active, dy, sides, groups)
    if swap:
        unit_sums = sum_chips(unit_grads.reshape((-1,) + unit_grads.shape[2:]), CHIPS)
        grad_units = to_cores(unit_sums)
    else:
        grad_units = scatter_rows(unit_grads)
    qkv, grad_att = qkv_call(one, dy, w_heads, qkv_shift, cos_lanes, sin_lanes, unit_grads)
    attended, dq, dk, dv = attend_call(begin, qkv, grad_att, doc, cos_rows, sin_rows)
    out_keep, out_send = output_call(core_scalar, span, attended, active, w_heads, w_units, unit_rows)

    bias_rows = out_biases.astype(F32)
    wide_x = own_x.astype(F32)
    residual = wide_x + bias_rows[0] + bias_rows[1]
    upstream = own_dy
    if sharing > 1:
        leader = tensor_index % sharing == 0
        residual = jnp.where(leader, residual, 0.0)
        upstream = jnp.where(leader, upstream, 0.0).astype(BF)
    out_part = out_keep + swap_cores(out_send).astype(F32)
    out_low = (residual + out_part).astype(BF)
    hidden_out = from_chip(out_low)

    head_grads = head_grads_call(dq, dk, dv, attended, one, dy, sides, out_low)
    e_keep, e_send, stats, qkv_sum = back_call(
        core_scalar, span, dq, dk, dv, grad_pre, x, w_heads, w_units, gains, unit_rows, head_grads
    )
    if swap:
        far = lax.dynamic_index_in_dim(head_grads, 1 - side, 0, keepdims=False)
        folded = fold_call(side.reshape(1), head_grads, side_swap(far), unit_sums)
        grad_heads = to_cores(sum_chips(folded, "tensor"))
    else:
        grad_heads = scatter_rows(head_grads)
    input_rows = finish_call(e_keep, swap_cores(e_send), own_x, upstream, hidden_out)
    input_grad = from_chip(input_rows)

    qkv_sum = qkv_sum.reshape(3, heads, HD).transpose(1, 0, 2).reshape(-1, 3 * HD)
    qkv_sum = place_pieces(qkv_sum)
    unit_sum = place_pieces(unit_sum.reshape(-1, unit_rows))
    out_sum = jnp.sum(out_grad.astype(F32), axis=(0, 1))
    packed = jnp.concatenate(
        [stats.reshape(-1), out_sum, qkv_sum.reshape(-1), unit_sum.reshape(-1)]
    )
    if swap:
        packed = packed + swap_cores(packed)
        packed = packed + side_swap(packed)
        bit = 1
        while bit < chips:
            packed = packed + lax.ppermute(packed, "tensor", [(i, i ^ bit) for i in range(chips)])
            bit *= 2
    else:
        packed = lax.psum(packed, EVERY)
    sums = packed[: 5 * feats].reshape(5, feats)
    qkv_size = chips * local_heads * 3 * HD
    qkv_all = packed[5 * feats : 5 * feats + qkv_size].reshape(chips, local_heads, 3 * HD)
    unit_all = packed[5 * feats + qkv_size :].reshape(chips, local_units)
    grad_qkv_b = lax.dynamic_index_in_dim(qkv_all, tensor_index, 0, keepdims=False)
    grad_unit_b = lax.dynamic_index_in_dim(unit_all, tensor_index, 0, keepdims=False)
    return (
        hidden_out,
        input_grad,
        sums[0:2],
        sums[2:4],
        grad_heads[:, : 3 * HD].transpose(2, 0, 1),
        grad_qkv_b,
        grad_heads[:, 3 * HD :],
        grad_units[:, :unit_rows].reshape(local_units, cols).T,
        grad_unit_b,
        grad_units[:, unit_rows:].reshape(local_units, cols),
        jnp.stack([sums[4], sums[4]]),
    )


def solution(mesh):
    rows = P("fsdp", ("tensor", "ctx"), None)
    weights = (
        P(("fsdp", "ctx"), "tensor", None),
        P("tensor", None),
        P("tensor", None, ("fsdp", "ctx")),
        P(("fsdp", "ctx"), "tensor"),
        P("tensor"),
        P("tensor", ("fsdp", "ctx")),
    )
    return jax.shard_map(
        body,
        mesh=mesh,
        in_specs=(rows, P("fsdp", None), P(), P()) + weights + (P(), rows),
        out_specs=(rows, rows, P(), P()) + weights + (P(),),
        check_vma=False,
    )
```

```python
import jax
import jax.numpy as jnp
import numpy as np
from jax import lax
from jax.experimental import pallas as pl
from jax.experimental.layout import Layout, with_layout_constraint
from jax.experimental.pallas import tpu as pltpu
from jax.sharding import PartitionSpec as P

HD = 64
ROT = 16
PAIR = 2 * HD
TILE = 256
WIDE = 512
SPAN = 1024
CHIPS = ("fsdp", "tensor")
EVERY = ("fsdp", "tensor", "ctx")
BF = jnp.bfloat16
F32 = jnp.float32
epsilon = 1e-05
VMEM = 56 * 1024 * 1024


AFTER = pl.BlockSpec(memory_space=pl.ANY)


def nt(a, b):
    return lax.dot_general(a, b, (((1,), (1,)), ((), ())), preferred_element_type=F32)


def nn(a, b):
    return jnp.dot(a, b, preferred_element_type=F32)


def tn(a, b):
    return lax.dot_general(a, b, (((0,), (0,)), ((), ())), preferred_element_type=F32)


def params(*kinds):
    return pltpu.CompilerParams(dimension_semantics=kinds, vmem_limit_bytes=VMEM)


def cost(flops, moved, special=0):
    return pl.CostEstimate(flops=int(flops), bytes_accessed=int(moved), transcendentals=int(special))


def layer_stats(values):
    center = values - jnp.mean(values, axis=-1, keepdims=True)
    inverse = lax.rsqrt(jnp.mean(center * center, axis=-1, keepdims=True) + epsilon)
    return (center * inverse, inverse)


def in_order(core_ref, own_ref, far_ref):
    first = core_ref[0] == 0
    own, far = own_ref[0], far_ref[0]
    return jnp.where(first, own, far), jnp.where(first, far, own)


def merge_kernel(core_ref, own_ref, far_ref, after_ref, out_ref):
    span = own_ref.shape[1]
    low, high = in_order(core_ref, own_ref, far_ref)
    out_ref[:span, :] = low
    out_ref[span:, :] = high


def norms_kernel(core_ref, own_ref, far_ref, gain_ref, shift_ref, out_ref, one_ref, two_ref):
    span = own_ref.shape[1]
    for index, rows in enumerate(in_order(core_ref, own_ref, far_ref)):
        place = slice(index * span, (index + 1) * span)
        out_ref[place, :] = rows
        normed, _ = layer_stats(rows.astype(F32))
        one_ref[place, :] = (normed * gain_ref[0:1, :] + shift_ref[0:1, :]).astype(BF)
        two_ref[place, :] = (normed * gain_ref[1:2, :] + shift_ref[1:2, :]).astype(BF)


def merge_call(core, own, far, after=None, gains=None, shifts=None):
    blocks, span, feats = own.shape
    tokens = 2 * blocks * span
    block = pl.BlockSpec((1, span, feats), lambda i, *_: (i, 0, 0))
    row = pl.BlockSpec((2 * span, feats), lambda i, *_: (i, 0))
    pair = pl.BlockSpec((2, feats), lambda i, *_: (0, 0))
    plain = gains is None
    count = 1 if plain else 3
    return pl.pallas_call(
        merge_kernel if plain else norms_kernel,
        grid_spec=pltpu.PrefetchScalarGridSpec(
            num_scalar_prefetch=1,
            grid=(blocks,),
            in_specs=[block, block] + ([AFTER] if plain else [pair, pair]),
            out_specs=[row] * count,
        ),
        out_shape=[jax.ShapeDtypeStruct((tokens, feats), BF)] * count,
        compiler_params=params("arbitrary"),
        cost_estimate=cost(tokens * feats * 12, tokens * feats * 2 * (1 + count)),
        name="merge" if plain else "norms",
    )(*((core, own, far) + ((after,) if plain else (gains, shifts))))


def block_of(ref, side, first, count):
    rows = ref[side, :, first : first + count, :]
    return rows.reshape(-1, rows.shape[-1])


def columns(side, wide):
    return slice(side * wide, (side + 1) * wide)


def qkv_kernel(
    one_ref, dy_ref, w_ref, bias_ref, cos_ref, sin_ref, lanes_ref, after_ref, out_ref, grad_ref
):
    sides, groups, _, wide = w_ref.shape
    width = groups * HD
    lane = lax.broadcasted_iota(jnp.int32, (WIDE, PAIR), 1) % HD
    low_half = lane < ROT // 2


    def spread(table_ref, first):
        table = jnp.concatenate([table_ref[i] for i in range(WIDE // TILE)], axis=1)
        return lax.dot_general(
            table,
            lanes_ref[first : first + ROT // 2, :],
            (((0,), (0,)), ((), ())),
            precision=lax.Precision.HIGHEST,
            preferred_element_type=F32,
        )

    cosine = spread(cos_ref, 0) + lanes_ref[ROT : ROT + 1, :]
    sine_part = spread(sin_ref, ROT // 2)

    def product(rows_ref, part):
        return sum(
            nt(rows_ref[:, columns(f, wide)], block_of(w_ref, f, part * HD, HD))
            for f in range(sides)
        )

    for part in range(3):
        span = slice(part * width, (part + 1) * width)
        whole = product(one_ref, part) + bias_ref[:, span]
        if part == 2:
            out_ref[:, span] = whole.astype(BF)
            continue
        for first in range(0, width, PAIR):
            u = whole[:, first : first + PAIR]
            turned = jnp.where(
                low_half, pltpu.roll(u, PAIR - ROT // 2, 1), pltpu.roll(u, ROT // 2, 1)
            )
            u = u * cosine + turned * sine_part
            if part == 0:
                u = u * HD ** (-0.5)
            out_ref[:, part * width + first : part * width + first + PAIR] = u.astype(BF)
    grad_ref[...] = product(dy_ref, 3).astype(BF)


def qkv_call(one, dy, w, bias, cosine, sine_part, lanes, after):
    tokens, feats = one.shape
    width = w.shape[1] * HD
    row = lambda size: pl.BlockSpec((WIDE, size), lambda i: (i, 0))
    table = pl.BlockSpec((WIDE // TILE, ROT // 2, TILE), lambda i: (i, 0, 0))
    return pl.pallas_call(
        qkv_kernel,
        grid=(tokens // WIDE,),
        in_specs=[
            row(feats),
            row(feats),
            pl.BlockSpec(w.shape, lambda i: (0, 0, 0, 0)),
            pl.BlockSpec((1, 3 * width), lambda i: (0, 0)),
            table,
            table,
            pl.BlockSpec(lanes.shape, lambda i: (0, 0)),
            AFTER,
        ],
        out_specs=[row(3 * width), row(width)],
        out_shape=[
            jax.ShapeDtypeStruct((tokens, 3 * width), BF),
            jax.ShapeDtypeStruct((tokens, width), BF),
        ],
        compiler_params=params("arbitrary"),
        cost_estimate=cost(16 * tokens * feats * width, 8 * tokens * (feats + width)),
        name="qkv",
    )(one, dy, w, bias, cosine, sine_part, lanes, after)


def turn_back(g, cosine, sine_part):
    eight = ROT // 2
    parts = []
    for head in range(2):
        own = g[head * HD : (head + 1) * HD]
        low, high = own[:eight], own[eight:ROT]
        parts += [low * cosine + high * sine_part, high * cosine - low * sine_part, own[ROT:]]
    return jnp.concatenate(parts, axis=0)


def attend_kernel(
    begin_ref,
    q_ref,
    k_ref,
    v_ref,
    grad_ref,
    doc_ref,
    cos_ref,
    sin_ref,
    att_ref,
    dq_ref,
    dk_ref,
    dv_ref,
    score_ref,
    prob_ref,
    key_turn_ref,
    value_turn_ref,
    dk_sum_ref,
    dv_sum_ref,
):
    tile = pl.program_id(1)
    tiles = pl.num_programs(1)
    total_tiles = k_ref.shape[0] // TILE

    @pl.when(tile == 0)
    def _():
        dk_sum_ref[...] = jnp.zeros_like(dk_sum_ref)
        dv_sum_ref[...] = jnp.zeros_like(dv_sum_ref)

        def turn(block, _):
            rows = pl.ds(pl.multiple_of(block * TILE, TILE), TILE)
            key_turn_ref[block] = k_ref[rows, :].astype(F32).T.astype(BF)
            value_turn_ref[block] = v_ref[rows, :].astype(F32).T.astype(BF)
            return 0

        lax.fori_loop(0, total_tiles, turn, 0)

    lane = lax.broadcasted_iota(jnp.int32, (TILE, PAIR), 1)
    q_wide = q_ref[...].astype(F32)
    g_wide = grad_ref[...].astype(F32)
    q_heads = [
        jnp.where(lane < HD, q_wide, 0.0).astype(BF),
        jnp.where(lane >= HD, q_wide, 0.0).astype(BF),
    ]
    g_heads = [
        jnp.where(lane < HD, g_wide, 0.0).astype(BF),
        jnp.where(lane >= HD, g_wide, 0.0).astype(BF),
    ]
    first = begin_ref[tile]
    doc = doc_ref[0]
    key_place = lax.broadcasted_iota(jnp.int32, (TILE, TILE), 0)
    query_place = lax.broadcasted_iota(jnp.int32, (TILE, TILE), 1) + tile * TILE

    def rows_of(block):
        return pl.ds(pl.multiple_of(block * TILE, TILE), TILE)

    def scores_step(block, tops):
        keys = k_ref[rows_of(block), :]
        place = key_place + block * TILE
        allowed = (place >= doc) & (place <= query_place)
        new = []
        for head in range(2):
            s = jnp.where(allowed, nt(keys, q_heads[head]), -1e30)
            score_ref[head, rows_of(block - first), :] = s
            new.append(jnp.maximum(tops[head], jnp.max(s, axis=0, keepdims=True)))
        return tuple(new)

    lowest = jnp.full((1, TILE), -1e30, F32)
    tops = lax.fori_loop(first, tile + 1, scores_step, (lowest, lowest))

    def exp_step(block, sums):
        values = v_ref[rows_of(block), :]
        new = []
        for head in range(2):
            e = jnp.exp(score_ref[head, rows_of(block - first), :] - tops[head])
            score_ref[head, rows_of(block - first), :] = e
            gp = nt(values, g_heads[head])
            prob_ref[head, rows_of(block - first), :] = gp
            new.append(sums[2 * head] + jnp.sum(e, axis=0, keepdims=True))
            new.append(sums[2 * head + 1] + jnp.sum(e * gp, axis=0, keepdims=True))
        return tuple(new)

    none = jnp.zeros((1, TILE), F32)
    sums = lax.fori_loop(first, tile + 1, exp_step, (none,) * 4)
    inverse = [1.0 / sums[0], 1.0 / sums[2]]
    means = [sums[1] * inverse[0], sums[3] * inverse[1]]

    def grad_step(block, turned):
        new = []
        dk = dk_sum_ref[rows_of(block), :]
        dv = dv_sum_ref[rows_of(block), :]
        for head in range(2):
            p = score_ref[head, rows_of(block - first), :] * inverse[head]
            gs = (p * (prob_ref[head, rows_of(block - first), :] - means[head])).astype(BF)
            p_low = p.astype(BF)
            dv = dv + nn(p_low, g_heads[head])
            dk = dk + nn(gs, q_heads[head])
            half = slice(head * HD, (head + 1) * HD)
            new.append(turned[2 * head] + nn(value_turn_ref[block, half, :], p_low))
            new.append(turned[2 * head + 1] + nn(key_turn_ref[block, half, :], gs))
        dk_sum_ref[rows_of(block), :] = dk
        dv_sum_ref[rows_of(block), :] = dv
        return tuple(new)

    flat = jnp.zeros((HD, TILE), F32)
    turned = lax.fori_loop(first, tile + 1, grad_step, (flat,) * 4)
    att_ref[...] = jnp.concatenate([turned[0], turned[2]], axis=0).T.astype(BF)
    dq = jnp.concatenate([turned[1], turned[3]], axis=0) * HD ** (-0.5)
    dq_ref[...] = turn_back(dq, cos_ref[tile], sin_ref[tile]).T.astype(BF)

    @pl.when(tile == tiles - 1)
    def _():
        dv_ref[...] = dv_sum_ref[...].astype(BF)

        def finish(block, _):
            g = dk_sum_ref[rows_of(block), :].T
            dk_ref[rows_of(block), :] = turn_back(g, cos_ref[block], sin_ref[block]).T.astype(BF)
            return 0

        lax.fori_loop(0, total_tiles, finish, 0)


def attend_call(begin, qkv, grad_att, doc, cosine, sine_part):
    tokens = qkv.shape[0]
    width = qkv.shape[1] // 3
    pairs = width // PAIR
    tiles = tokens // TILE
    reach = SPAN + TILE
    query = pl.BlockSpec((TILE, PAIR), lambda p, i, *_: (i, p))
    whole = pl.BlockSpec((tokens, PAIR), lambda p, i, *_: (0, p))
    table = pl.BlockSpec((tiles, ROT // 2, TILE), lambda p, i, *_: (0, 0, 0))
    return pl.pallas_call(
        attend_kernel,
        grid_spec=pltpu.PrefetchScalarGridSpec(
            num_scalar_prefetch=1,
            grid=(pairs, tiles),
            in_specs=[
                query,
                pl.BlockSpec((tokens, PAIR), lambda p, i, *_: (0, pairs + p)),
                pl.BlockSpec((tokens, PAIR), lambda p, i, *_: (0, 2 * pairs + p)),
                query,
                pl.BlockSpec((1, 1, TILE), lambda p, i, *_: (i, 0, 0)),
                table,
                table,
            ],
            out_specs=[query, query, whole, whole],
            scratch_shapes=[
                pltpu.VMEM((2, reach, TILE), F32),
                pltpu.VMEM((2, reach, TILE), F32),
                pltpu.VMEM((tiles, PAIR, TILE), BF),
                pltpu.VMEM((tiles, PAIR, TILE), BF),
                pltpu.VMEM((tokens, PAIR), F32),
                pltpu.VMEM((tokens, PAIR), F32),
            ],
        ),
        out_shape=[jax.ShapeDtypeStruct((tokens, width), BF)] * 4,
        compiler_params=params("arbitrary", "arbitrary"),
        cost_estimate=cost(
            tokens * 800 * width * 4 * 12, tokens * width * 16, tokens * 600 * (width // HD)
        ),
        name="attend",
    )(begin, qkv, qkv, qkv, grad_att, doc, cosine, sine_part)


def normal(v):
    bell = jnp.exp(-0.5 * v * v)
    t = 1.0 / (1.0 + 0.2316418882 * jnp.abs(v))
    tail = 0.7107068705 + t * (-0.7265760135 + t * 0.5307027145)
    tail = 0.127414796 + t * (-0.142248368 + t * tail)
    tail = jnp.where(v < 0, 1.0, -1.0) * (t * tail * bell)
    return jnp.where(v < 0, 0.0, 1.0) + tail, bell * 0.3989422804014327


def units_kernel(two_ref, dy_ref, win_ref, wout_ref, bias_ref, act_ref, pre_ref, sum_ref):
    sides, _, rows, wide = win_ref.shape
    pre = bias_ref[...]
    upstream = 0.0
    for f in range(sides):
        pre = pre + nt(two_ref[:, columns(f, wide)], block_of(win_ref, f, 0, rows))
        upstream = upstream + nt(dy_ref[:, columns(f, wide)], block_of(wout_ref, f, 0, rows))
    cdf, density = normal(pre)
    act_ref[...] = (pre * cdf).astype(BF)
    back = (upstream * (cdf + pre * density)).astype(BF)
    pre_ref[...] = back

    @pl.when(pl.program_id(1) == 0)
    def _():
        sum_ref[...] = jnp.zeros_like(sum_ref)

    sum_ref[...] += jnp.sum(back.astype(F32), axis=0, keepdims=True)


def units_call(two, dy, w, bias, rows):
    tokens, feats = two.shape
    sides, groups, _, wide = w.shape
    units = groups * rows
    taken = max(1, 512 // rows)
    step = taken * rows
    row = pl.BlockSpec((WIDE, feats), lambda j, i: (i, 0))
    line = pl.BlockSpec((1, step), lambda j, i: (0, j))
    out = pl.BlockSpec((WIDE, step), lambda j, i: (i, j))
    return pl.pallas_call(
        units_kernel,
        grid=(units // step, tokens // WIDE),
        in_specs=[
            row,
            row,
            pl.BlockSpec((sides, taken, rows, wide), lambda j, i: (0, j, 0, 0)),
            pl.BlockSpec((sides, taken, rows, wide), lambda j, i: (0, j, 1, 0)),
            line,
        ],
        out_specs=[out, out, line],
        out_shape=[
            jax.ShapeDtypeStruct((tokens, units), BF),
            jax.ShapeDtypeStruct((tokens, units), BF),
            jax.ShapeDtypeStruct((1, units), F32),
        ],
        compiler_params=params("arbitrary", "arbitrary"),
        cost_estimate=cost(10 * tokens * feats * units, 40 * tokens * feats, 2 * tokens * units),
        name="units",
    )(two, dy, w, w, bias)


def unit_grads_kernel(pre_ref, two_ref, act_ref, dy_ref, out_ref):
    _, taken, rows, wide = out_ref.shape
    rows = rows // 2
    got = tn(pre_ref[...], two_ref[...]).astype(BF)
    out_ref[0, :, :rows, :] = got.reshape(taken, rows, wide)
    got = tn(act_ref[...], dy_ref[...]).astype(BF)
    out_ref[0, :, rows:, :] = got.reshape(taken, rows, wide)


def unit_grads_call(pre, two, act, dy, sides, groups):
    tokens, feats = two.shape
    units = act.shape[1]
    rows, wide = units // groups, feats // sides
    taken = max(1, 512 // rows)
    left = pl.BlockSpec((tokens, taken * rows), lambda f, t: (0, t))
    right = pl.BlockSpec((tokens, wide), lambda f, t: (0, f))
    return pl.pallas_call(
        unit_grads_kernel,
        grid=(sides, groups // taken),
        in_specs=[left, right, left, right],
        out_specs=pl.BlockSpec((1, taken, 2 * rows, wide), lambda f, t: (f, t, 0, 0)),
        out_shape=jax.ShapeDtypeStruct((sides, groups, 2 * rows, wide), BF),
        compiler_params=params("arbitrary", "arbitrary"),
        cost_estimate=cost(6 * tokens * feats * units, 4 * tokens * (feats + 2 * units)),
        name="unit_grads",
    )(pre, two, act, dy)


def head_grads_kernel(order_ref, dq_ref, dk_ref, dv_ref, att_ref, one_ref, dy_ref, *out_refs):
    pairs = ((dq_ref, one_ref), (dk_ref, one_ref), (dv_ref, one_ref), (att_ref, dy_ref))
    for step, out_ref in enumerate(out_refs):
        groups, _, wide = out_ref.shape

        @pl.when(pl.program_id(0) == step)
        def _():
            for part, (left, right) in enumerate(pairs):
                got = tn(left[...], right[...]).astype(BF)
                out_ref[:, part * HD : (part + 1) * HD, :] = got.reshape(groups, HD, wide)


def head_grads_call(order, dq, dk, dv, att, one, dy):
    tokens, feats = one.shape
    width = dq.shape[1]
    sides = order.shape[0]
    groups, wide = width // HD, feats // sides
    left = pl.BlockSpec((tokens, width), lambda i, *_: (0, 0))
    right = pl.BlockSpec((tokens, wide), lambda i, order_ref: (0, order_ref[i]))
    shape = (groups, 4 * HD, wide)
    return pl.pallas_call(
        head_grads_kernel,
        grid_spec=pltpu.PrefetchScalarGridSpec(
            num_scalar_prefetch=1,
            grid=(sides,),
            in_specs=[left] * 4 + [right] * 2,
            out_specs=[pl.BlockSpec(shape, lambda i, *_: (0, 0, 0))] * sides,
        ),
        out_shape=[jax.ShapeDtypeStruct(shape, BF)] * sides,
        compiler_params=params("arbitrary"),
        cost_estimate=cost(12 * tokens * feats * width, 4 * tokens * (feats + 2 * width)),
        name="head_grads",
    )(order, dq, dk, dv, att, one, dy)


def keep_and_send(core_ref, whole, keep_ref, send_ref, place):
    blocks, span, _ = keep_ref.shape
    first = core_ref[0] == 0
    for block in range(blocks):
        at = 2 * block * span
        low, high = whole[at : at + span], whole[at + span : at + 2 * span]
        keep_ref[block, :, place] = jnp.where(first, low, high)
        send_ref[block, :, place] = jnp.where(first, high, low).astype(BF)


def shared_specs(blocks, span, feats):
    block = pl.BlockSpec((WIDE // (2 * span), span, feats), lambda i, *_: (i, 0, 0))
    shape = (blocks, span, feats)
    return [block, block], [jax.ShapeDtypeStruct(shape, F32), jax.ShapeDtypeStruct(shape, BF)]


def output_kernel(core_ref, att_ref, act_ref, wd_ref, wout_ref, after_ref, keep_ref, send_ref):
    sides, _, rows, wide = wout_ref.shape
    for f in range(sides):
        whole = nn(att_ref[...], block_of(wd_ref, f, 0, HD))
        whole += nn(act_ref[...], block_of(wout_ref, f, 0, rows))
        keep_and_send(core_ref, whole, keep_ref, send_ref, columns(f, wide))


def output_call(core, span, att, act, w_heads, w_units, rows, after):
    tokens, width = att.shape
    units = act.shape[1]
    sides, groups, _, wide = w_units.shape
    feats = sides * wide
    step = WIDE
    specs, shapes = shared_specs(tokens // (2 * span), span, feats)
    return pl.pallas_call(
        output_kernel,
        grid_spec=pltpu.PrefetchScalarGridSpec(
            num_scalar_prefetch=1,
            grid=(tokens // step,),
            in_specs=[
                pl.BlockSpec((step, width), lambda i, *_: (i, 0)),
                pl.BlockSpec((step, units), lambda i, *_: (i, 0)),
                pl.BlockSpec((sides, groups, HD, wide), lambda i, *_: (0, 0, 3, 0)),
                pl.BlockSpec((sides, groups, rows, wide), lambda i, *_: (0, 0, 1, 0)),
                AFTER,
            ],
            out_specs=specs,
        ),
        out_shape=shapes,
        compiler_params=params("arbitrary"),
        cost_estimate=cost(
            3 * tokens * feats * (width + units),
            2 * (tokens * (width + units + 2 * feats) + feats * (width + units)),
        ),
        name="output",
    )(core, att, act, w_heads, w_units, after)


def back_kernel(
    core_ref,
    dq_ref,
    dk_ref,
    dv_ref,
    pre_ref,
    x_ref,
    w_ref,
    win_ref,
    gain_ref,
    after_ref,
    keep_ref,
    send_ref,
    stat_ref,
    bias_ref,
):
    width = dq_ref.shape[1]
    sides, _, rows, wide = win_ref.shape
    parts = [dq_ref[...], dk_ref[...], dv_ref[...]]
    normed, _ = layer_stats(x_ref[...].astype(F32))

    @pl.when(pl.program_id(0) == 0)
    def _():
        stat_ref[...] = jnp.zeros_like(stat_ref)
        bias_ref[...] = jnp.zeros_like(bias_ref)

    for f in range(sides):
        place = columns(f, wide)
        one = sum(nn(part, block_of(w_ref, f, at * HD, HD)) for at, part in enumerate(parts))
        two = nn(pre_ref[...], block_of(win_ref, f, 0, rows))
        whole = one * gain_ref[0:1, place] + two * gain_ref[1:2, place]
        keep_and_send(core_ref, whole, keep_ref, send_ref, place)
        n = normed[:, place]
        for row, value in enumerate((one * n, two * n, one, two)):
            stat_ref[row : row + 1, place] += jnp.sum(value, axis=0, keepdims=True)
    for row in range(3):
        span = slice(row * width, (row + 1) * width)
        bias_ref[:, span] += jnp.sum(parts[row].astype(F32), axis=0, keepdims=True)


def back_call(core, span, dq, dk, dv, pre, x, w_heads, w_units, gains, rows, after):
    tokens, width = dq.shape
    units = pre.shape[1]
    sides, groups, _, wide = w_units.shape
    feats = sides * wide
    step = WIDE
    part = pl.BlockSpec((step, width), lambda i, *_: (i, 0))
    specs, shapes = shared_specs(tokens // (2 * span), span, feats)
    return pl.pallas_call(
        back_kernel,
        grid_spec=pltpu.PrefetchScalarGridSpec(
            num_scalar_prefetch=1,
            grid=(tokens // step,),
            in_specs=[
                part,
                part,
                part,
                pl.BlockSpec((step, units), lambda i, *_: (i, 0)),
                pl.BlockSpec((step, feats), lambda i, *_: (i, 0)),
                pl.BlockSpec(w_heads.shape, lambda i, *_: (0, 0, 0, 0)),
                pl.BlockSpec((sides, groups, rows, wide), lambda i, *_: (0, 0, 0, 0)),
                pl.BlockSpec((2, feats), lambda i, *_: (0, 0)),
                AFTER,
            ],
            out_specs=specs
            + [
                pl.BlockSpec((4, feats), lambda i, *_: (0, 0)),
                pl.BlockSpec((1, 3 * width), lambda i, *_: (0, 0)),
            ],
        ),
        out_shape=shapes
        + [
            jax.ShapeDtypeStruct((4, feats), F32),
            jax.ShapeDtypeStruct((1, 3 * width), F32),
        ],
        compiler_params=params("arbitrary"),
        cost_estimate=cost(
            3 * tokens * feats * (3 * width + units),
            2 * (tokens * (3 * width + units + 3 * feats) + feats * (3 * width + units)),
        ),
        name="back",
    )(core, dq, dk, dv, pre, x, w_heads, w_units, gains, after)


def fold_kernel(own_ref, far_ref, after_ref, out_ref):
    out_ref[...] = (own_ref[...].astype(F32) + far_ref[...].astype(F32)).astype(BF)


def fold_call(own, far, after):
    block = pl.BlockSpec((1,) + own.shape[1:], lambda i: (i, 0, 0))
    return pl.pallas_call(
        fold_kernel,
        grid=(own.shape[0],),
        in_specs=[block, block, AFTER],
        out_specs=block,
        out_shape=jax.ShapeDtypeStruct(own.shape, BF),
        compiler_params=params("arbitrary"),
        cost_estimate=cost(own.size * 2, own.size * 6),
        name="fold",
    )(own, far, after)


def finish_kernel(keep_ref, far_ref, x_ref, dy_ref, after_ref, out_ref):
    e = keep_ref[0] + far_ref[0].astype(F32)
    normed, inverse = layer_stats(x_ref[0].astype(F32))
    through = inverse * (
        e
        - jnp.mean(e, axis=-1, keepdims=True)
        - normed * jnp.mean(e * normed, axis=-1, keepdims=True)
    )
    out_ref[0] = (dy_ref[0].astype(F32) + through).astype(BF)


def finish_call(keep, far, x, dy, after):
    block = pl.BlockSpec((1,) + keep.shape[1:], lambda i: (i, 0, 0))
    return pl.pallas_call(
        finish_kernel,
        grid=(keep.shape[0],),
        in_specs=[block] * 4 + [AFTER],
        out_specs=block,
        out_shape=jax.ShapeDtypeStruct(keep.shape, BF),
        compiler_params=params("arbitrary"),
        cost_estimate=cost(keep.size * 20, keep.size * 12),
        name="finish",
    )(keep, far, x, dy, after)


def swap_cores(v):
    return lax.ppermute(v, "ctx", [(0, 1), (1, 0)])


def body(
    hidden_in,
    segment_ids,
    norm_gains,
    norm_biases,
    qkv_weight,
    qkv_bias,
    dense_weight,
    fc_in_weight,
    fc_in_bias,
    fc_out_weight,
    out_biases,
    out_grad,
):
    chips = lax.axis_size("tensor")
    rows_of_chips = lax.axis_size("fsdp")
    tensor_index = lax.axis_index("tensor")
    core = lax.axis_index("ctx")
    side = lax.axis_index("fsdp")
    local_seqs, span, feats = hidden_in.shape
    sharing = chips // local_seqs
    ranks = 2 * sharing
    tokens = 2 * chips * span
    tiles = tokens // TILE
    local_heads = qkv_bias.shape[0]
    local_units = fc_in_bias.shape[0]
    cols = qkv_weight.shape[0]
    own_seq = tensor_index // sharing
    rank = (tensor_index % sharing) * 2 + core
    swap = (
        sharing == 1 and local_heads == 2 and rows_of_chips == 2 and chips & (chips - 1) == 0
    )
    heads = chips * local_heads // ranks
    units = chips * local_units // ranks
    gains = norm_gains.astype(F32)
    shifts = norm_biases.astype(F32)
    core_scalar = core.reshape(1)

    def to_chip(rows):
        if sharing > 1:
            rows = jnp.repeat(rows, sharing, axis=0)
        return lax.all_to_all(rows, "tensor", 0, 0, tiled=True)

    def from_chip(rows):
        rows = lax.all_to_all(rows, "tensor", 0, 0, tiled=True)
        if sharing > 1:
            rows = rows.reshape(local_seqs, sharing, span, feats).astype(F32)
            rows = jnp.sum(rows, axis=1).astype(BF)
        return rows

    def ordered(own, far, axis):
        return jnp.where(
            core == 0,
            jnp.concatenate([own, far], axis=axis),
            jnp.concatenate([far, own], axis=axis),
        )

    def gather_rows(shard, extra=None):
        rows = shard.shape[1]
        if swap:
            own = lax.dynamic_index_in_dim(shard, core, 0, keepdims=False)
            far = lax.dynamic_index_in_dim(shard, 1 - core, 0, keepdims=False)
            mine = ordered(own, swap_cores(far), 1)
            if extra is not None:
                mine = jnp.concatenate([mine, extra])
            full = lax.all_gather(mine, CHIPS, axis=0, tiled=False)
            return full.reshape((rows_of_chips, chips) + mine.shape)
        full = lax.all_gather(shard.reshape(pieces * rows, cols), EVERY, axis=0, tiled=False)
        full = full.reshape(rows_of_chips, chips, 2, pieces, rows, cols)
        full = full.transpose(1, 3, 4, 0, 2, 5).reshape(1, chips * pieces, rows, feats)
        count = chips * pieces // ranks
        return lax.dynamic_slice_in_dim(full, rank * count, count, 1)

    def side_swap(v):
        return lax.ppermute(v, "fsdp", [(0, 1), (1, 0)])

    def sum_chips(full, axes):
        mine = lax.psum_scatter(full, axes, scatter_dimension=0, tiled=True)
        return with_layout_constraint(mine, Layout((0, 1, 2)))

    def to_cores(mine):
        mine = mine.reshape(-1, 2, cols)
        own = lax.dynamic_index_in_dim(mine, core, 1, keepdims=False)
        far = lax.dynamic_index_in_dim(mine, 1 - core, 1, keepdims=False)
        return ordered(own[None], swap_cores(far)[None], 0).astype(F32)

    def scatter_rows(full):
        rows = full.shape[2]
        wide = jnp.zeros((chips * pieces, rows, feats), BF)
        wide = lax.dynamic_update_slice_in_dim(wide, full[0], rank * full.shape[1], 0)
        wide = wide.reshape(chips, pieces, rows, rows_of_chips, 2, cols)
        wide = wide.transpose(3, 0, 4, 1, 2, 5).reshape(-1, pieces * rows, cols)
        mine = lax.psum_scatter(wide, EVERY, scatter_dimension=0, tiled=True)
        return mine.reshape(pieces, rows, cols).astype(F32)

    def own_pieces(full):
        full = full.reshape((chips * pieces,) + full.shape[2:])
        count = chips * pieces // ranks
        return lax.dynamic_slice_in_dim(full, rank * count, count, 0)

    def place_pieces(part):
        size = part.shape[1]
        if swap:
            wide = jnp.zeros((chips, pieces, size), F32)
            return lax.dynamic_update_slice_in_dim(wide, part[:, None], core, 1)
        wide = jnp.zeros((chips * pieces, size), F32)
        wide = lax.dynamic_update_slice_in_dim(wide, part, rank * part.shape[0], 0)
        return wide.reshape(chips, pieces, size)

    pieces = local_heads
    unit_rows = local_units // pieces
    unit_shards = jnp.concatenate(
        [
            fc_in_weight.T.reshape(pieces, unit_rows, cols),
            fc_out_weight.reshape(pieces, unit_rows, cols),
        ],
        axis=1,
    )
    head_shards = jnp.concatenate([qkv_weight.transpose(1, 2, 0), dense_weight], axis=1)

    own_x = to_chip(hidden_in)
    own_dy = to_chip(out_grad)
    if swap:
        shift_row = jnp.concatenate(
            [
                lax.dynamic_index_in_dim(qkv_bias, core, 0, keepdims=False),
                lax.dynamic_slice_in_dim(fc_in_bias, core * unit_rows, unit_rows, 0),
            ]
        )
        shift_rows = jnp.zeros((16, 2 * cols), BF)
        shift_rows = lax.dynamic_update_slice(shift_rows, shift_row[None], (0, 0))
        w_units = gather_rows(unit_shards, shift_rows)
        bias_all = w_units[0, :, 2 * unit_rows, :].astype(F32)
        w_heads = gather_rows(head_shards)
        qkv_shift = bias_all[:, : 3 * HD]
        unit_shift = bias_all[:, 3 * HD : 3 * HD + unit_rows]
    else:
        bias_vector = jnp.concatenate([qkv_bias.reshape(-1), fc_in_bias]).astype(F32)
        bias_all = lax.all_gather(bias_vector, "tensor", axis=0, tiled=False)
        qkv_size = local_heads * 3 * HD
        qkv_shift = own_pieces(bias_all[:, :qkv_size].reshape(chips, pieces, 3 * HD))
        unit_shift = own_pieces(bias_all[:, qkv_size:].reshape(chips, pieces, unit_rows))
        w_units = gather_rows(unit_shards)
        w_heads = gather_rows(head_shards)
    qkv_shift = qkv_shift.reshape(heads, 3, HD).transpose(1, 0, 2).reshape(1, -1)
    unit_shift = unit_shift.reshape(1, units)
    sides, groups = w_units.shape[:2]

    segments = lax.dynamic_index_in_dim(segment_ids, own_seq, 0, keepdims=False)
    places = lax.broadcasted_iota(jnp.int32, (tokens,), 0)
    change = jnp.concatenate(
        [jnp.ones((1,), jnp.int32), (segments[1:] != segments[:-1]).astype(jnp.int32)]
    )
    starts = lax.cummax(places * change, axis=0)
    begin = starts[::TILE] // TILE
    freqs = 10000.0 ** (-jnp.arange(0, ROT, 2, dtype=F32) / ROT)
    angle = (places - starts).astype(F32).reshape(tiles, 1, TILE) * freqs[:, None]
    cos_rows, sin_rows = jnp.cos(angle), jnp.sin(angle)
    lane = np.arange(PAIR) % HD
    spot = np.arange(ROT // 2)[:, None] == lane % (ROT // 2)
    turning = lane < ROT
    signs = np.where(lane < ROT // 2, -1.0, 1.0)
    lanes = np.zeros((24, PAIR), np.float32)
    lanes[: ROT // 2] = spot & turning
    lanes[ROT // 2 : ROT] = (spot & turning) * signs
    lanes[ROT] = ~turning
    lanes = jnp.asarray(lanes)

    doc = starts.reshape(tiles, 1, TILE)
    x, one, two = merge_call(core_scalar, own_x, swap_cores(own_x), None, gains, shifts)
    (dy,) = merge_call(core_scalar, own_dy, swap_cores(own_dy), one)
    active, grad_pre, unit_sum = units_call(two, dy, w_units, unit_shift, unit_rows)
    unit_grads = unit_grads_call(grad_pre, two, active, dy, sides, groups)
    if swap:
        unit_sums = sum_chips(unit_grads.reshape((-1,) + unit_grads.shape[2:]), CHIPS)
        grad_units = to_cores(unit_sums)
    else:
        grad_units = scatter_rows(unit_grads)
    qkv, grad_att = qkv_call(one, dy, w_heads, qkv_shift, cos_rows, sin_rows, lanes, unit_grads)
    attended, dq, dk, dv = attend_call(begin, qkv, grad_att, doc, cos_rows, sin_rows)
    order = jnp.stack([1 - side, side]) if swap else jnp.zeros((1,), jnp.int32)
    head_grads = head_grads_call(order, dq, dk, dv, attended, one, dy)
    if swap:
        far = side_swap(head_grads[0])
    out_keep, out_send = output_call(
        core_scalar, span, attended, active, w_heads, w_units, unit_rows, head_grads[0]
    )

    bias_rows = out_biases.astype(F32)
    wide_x = own_x.astype(F32)
    residual = wide_x + bias_rows[0] + bias_rows[1]
    upstream = own_dy
    if sharing > 1:
        leader = tensor_index % sharing == 0
        residual = jnp.where(leader, residual, 0.0)
        upstream = jnp.where(leader, upstream, 0.0).astype(BF)
    out_part = out_keep + swap_cores(out_send).astype(F32)
    out_low = (residual + out_part).astype(BF)
    hidden_out = from_chip(out_low)

    e_keep, e_send, stats, qkv_sum = back_call(
        core_scalar, span, dq, dk, dv, grad_pre, x, w_heads, w_units, gains, unit_rows, out_low
    )
    if swap:
        folded = fold_call(head_grads[1], far, unit_sums)
        grad_heads = to_cores(sum_chips(folded, "tensor"))
    else:
        grad_heads = scatter_rows(head_grads[0][None])
    input_rows = finish_call(e_keep, swap_cores(e_send), own_x, upstream, hidden_out)
    input_grad = from_chip(input_rows)

    qkv_sum = qkv_sum.reshape(3, heads, HD).transpose(1, 0, 2).reshape(-1, 3 * HD)
    qkv_sum = place_pieces(qkv_sum)
    unit_sum = place_pieces(unit_sum.reshape(-1, unit_rows))
    out_sum = jnp.sum(out_grad.astype(F32), axis=(0, 1))
    packed = jnp.concatenate(
        [stats.reshape(-1), out_sum, qkv_sum.reshape(-1), unit_sum.reshape(-1)]
    )
    if swap:
        packed = packed + swap_cores(packed)
        packed = packed + side_swap(packed)
        bit = 1
        while bit < chips:
            packed = packed + lax.ppermute(packed, "tensor", [(i, i ^ bit) for i in range(chips)])
            bit *= 2
    else:
        packed = lax.psum(packed, EVERY)
    sums = packed[: 5 * feats].reshape(5, feats)
    qkv_size = chips * local_heads * 3 * HD
    qkv_all = packed[5 * feats : 5 * feats + qkv_size].reshape(chips, local_heads, 3 * HD)
    unit_all = packed[5 * feats + qkv_size :].reshape(chips, local_units)
    grad_qkv_b = lax.dynamic_index_in_dim(qkv_all, tensor_index, 0, keepdims=False)
    grad_unit_b = lax.dynamic_index_in_dim(unit_all, tensor_index, 0, keepdims=False)
    return (
        hidden_out,
        input_grad,
        sums[0:2],
        sums[2:4],
        grad_heads[:, : 3 * HD].transpose(2, 0, 1),
        grad_qkv_b,
        grad_heads[:, 3 * HD :],
        grad_units[:, :unit_rows].reshape(local_units, cols).T,
        grad_unit_b,
        grad_units[:, unit_rows:].reshape(local_units, cols),
        jnp.stack([sums[4], sums[4]]),
    )


def solution(mesh):
    rows = P("fsdp", ("tensor", "ctx"), None)
    weights = (
        P(("fsdp", "ctx"), "tensor", None),
        P("tensor", None),
        P("tensor", None, ("fsdp", "ctx")),
        P(("fsdp", "ctx"), "tensor"),
        P("tensor"),
        P("tensor", ("fsdp", "ctx")),
    )
    return jax.shard_map(
        body,
        mesh=mesh,
        in_specs=(rows, P("fsdp", None), P(), P()) + weights + (P(), rows),
        out_specs=(rows, rows, P(), P()) + weights + (P(),),
        check_vma=False,
    )
```
